256 devices in a mesh: lat: 8 (over z_hi, core), lon: 32 (over y, z_lo, x).
Axes of the slice: x: 4, y: 4, z: 8 (z_hi: 4, z_lo: 2; z = z_hi * 2 + z_lo), core: 2. Of those that a mesh axis runs over, the one named last changes fastest.
Arguments:
- atm_state: bfloat16 [512, 1024, 384], P('lat', 'lon'), may hold values from -6 to 6
- atm_gain: float32 [384], replicated, may hold values from 0.1 to 1.9
- spec_weight: bfloat16 [2, 384, 384], replicated, may hold values from -0.21875 to 0.21875
- mlp_in: bfloat16 [384, 768], replicated, may hold values from -0.3125 to 0.3125
- mlp_out: bfloat16 [768, 384], replicated, may hold values from -0.21875 to 0.21875
- flux_weight: bfloat16 [384, 128], replicated, may hold values from -0.3125 to 0.3125
- return_weight: bfloat16 [128, 384], replicated, may hold values from -2 to 2
- ocean_state: bfloat16 [128, 512, 256], P('lat', 'lon'), may hold values from -6 to 6
- wet: int32 [128, 512], P('lat', 'lon'), may hold values 0 or 1
- ocean_in: bfloat16 [128, 256], replicated, may hold values from -0.5 to 0.5
- depth_kernel: bfloat16 [7, 7, 256], replicated, may hold values from -0.875 to 0.875
- ocean_gain: float32 [256], replicated, may hold values from 0.5 to 1.5
- ocean_up: bfloat16 [256, 1024], replicated, may hold values from -0.375 to 0.375
- ocean_down: bfloat16 [1024, 256], replicated, may hold values from -0.5 to 0.5
- surface_weight: bfloat16 [256, 128], replicated, may hold values from -0.375 to 0.375
- intersection_point: int32 [128, 512, 4], P('lat', 'lon'), may hold values from 16 to 4079, as said below
- intersection_weight: float32 [128, 512, 4], P('lat', 'lon'), may hold values from 0.1 to 1
- return_intersection: float32 [128, 512, 4], P('lat', 'lon'), may hold values from 0.1 to 1
- ocean_cot: bfloat16 [128, 512, 256], P('lat', 'lon'), may hold values from -0.15625 to 0.15625
Outputs:
- atm_next: bfloat16 [512, 1024, 384], P('lat', 'lon')
- ocean_next: bfloat16 [128, 512, 256], P('lat', 'lon')
- grad_up: float32 [256, 1024], replicated
- grad_down: float32 [1024, 256], replicated
The draws below stay inside these ranges and needn't reach their ends.
Inputs may be any that keep to these rules, and one draw needn't show every extreme that they name: `intersection_point`: A value j < 2048 is point j (numbered row by row) of the atmosphere block at the tile's own position; a larger j is point j - 2048 of the block one device further along lon (wrapping), always in that block's first 16 columns.
All inputs are finite; a program needn't handle non-finite values. No bound on the sum of `wet` on one device may be relied on, other than what follows from the above.
Results may differ from the reference program's by a relative error of at most 0.015.
Values may be sent and summed in bfloat16 or wider, within the bound.
No kernel may reach another device: no remote copies, remote signals or barrier semaphores. Data moves between devices by JAX's collectives and lax.ppermute only.
A program may use at most 128 MiB of HBM per device.

```python
import math
import jax
import jax.numpy as jnp
from jax import lax

C = 384
HID = 768
NLAT = 512
NLON = 1024
MW = 512
FL = 128
OC = 256
OH = 1024
ORW = 16
OCL = 16
KOV = 4
LAT_DEV = 64
LON_DEV = 32
ONR = 128
ONC = 512
N_LON = 32


def draw_intersection_point(key, part):
    key = jax.random.fold_in(key, 7)
    row_key, col_key = jax.random.split(key, 2)
    layout = (ONR, ONC, KOV)
    row_span = LAT_DEV // ORW
    col_span = LON_DEV // OCL
    local_row = (jnp.arange(ONR, dtype=jnp.int32) % ORW)[:, None, None]
    local_col = (jnp.arange(ONC, dtype=jnp.int32) % OCL)[None, :, None]
    intersection_ids = jnp.arange(KOV, dtype=jnp.int32)[None, None, :]
    row_off = jax.random.randint(row_key, layout, 0, row_span)
    col_off = jax.random.randint(col_key, layout, 0, col_span)
    first_cell = (local_row == 0) & (local_col == 0) & (intersection_ids == 0)
    last_cell = (local_row == ORW - 1) & (local_col == OCL - 1) & (intersection_ids == KOV - 1)
    row_off = jnp.where(first_cell, 0, jnp.where(last_cell, row_span - 1, row_off))
    col_off = jnp.where(first_cell, 0, jnp.where(last_cell, col_span - 1, col_off))
    atm_row = local_row * row_span + row_off
    atm_col = local_col * col_span + LON_DEV // 2 + col_off
    block_cells = LAT_DEV * LON_DEV
    own_point = atm_row * LON_DEV + atm_col
    east_point = block_cells + atm_row * LON_DEV + atm_col - LON_DEV
    return jnp.where(atm_col < LON_DEV, own_point, east_point).astype(jnp.int32)


def set_ends(values, own_key, smallest, top_value):
    index_at = [jax.random.randint(jax.random.fold_in(own_key, axis), (), 0, length) for axis, length in enumerate(values.shape)]
    main_axis = values.shape.index(max(values.shape))
    next_to = index_at[:main_axis] + [(index_at[main_axis] + 1) % values.shape[main_axis]] + index_at[main_axis + 1:]
    return values.at[tuple(index_at)].set(smallest).at[tuple(next_to)].set(top_value)


def steps_of(rng, dims, shards, least, top_value):
    loudness, own = 1.0, jax.random.fold_in(rng, 6)
    for axis_at, shards_of in shards:
        heights = jnp.exp(jax.random.uniform(jax.random.fold_in(own, axis_at), (shards_of,), jnp.float32, least / len(shards), top_value / len(shards)))
        loudness = loudness * jnp.repeat(heights, dims[axis_at] // shards_of).reshape([-1 if axis == axis_at else 1 for axis in range(len(dims))])
    return loudness


def normal_values(own_key, extent, scale, limit, shards=(), kind=jnp.bfloat16):
    drawn = jax.random.normal(own_key, extent, jnp.float32) * scale
    if len(shards) > 0:
        drawn = steps_of(own_key, extent, shards, -0.22, 0.18) * drawn
    return jnp.clip(drawn, min=-limit, max=limit).astype(kind)


def setup_inputs(seed: int = 0) -> dict:
    key_list = jax.random.split(jax.random.key(seed), 20)
    return {
        "atm_state": normal_values(key_list[0], (NLAT, NLON, C), 1.0, 6.0, ((0, 8), (1, 32))),
        "atm_gain": jnp.clip(1.0 + 0.18 * jax.random.normal(key_list[1], (C,), jnp.float32), 0.1, 1.9),
        "spec_weight": normal_values(key_list[2], (2, C, C), (2 * C) ** -0.5, 0.21875),
        "mlp_in": normal_values(key_list[3], (C, HID), C ** -0.5, 0.3125),
        "mlp_out": normal_values(key_list[4], (HID, C), HID ** -0.5, 0.21875),
        "flux_weight": normal_values(key_list[5], (C, FL), C ** -0.5, 0.3125),
        "return_weight": normal_values(key_list[6], (FL, C), (FL // 16) ** -0.5, 2.0),
        "ocean_state": normal_values(key_list[7], (ONR, ONC, OC), 1.0, 6.0, ((0, 8), (1, 32))),
        "wet": set_ends((jax.random.randint(key_list[8], (ONR, ONC), 0, 4) < 3).astype(jnp.int32), jax.random.fold_in(key_list[8], 1), 0, 1),
        "ocean_in": normal_values(key_list[9], (FL, OC), FL ** -0.5, 0.5),
        "depth_kernel": normal_values(key_list[10], (7, 7, OC), 49 ** -0.5, 0.875),
        "ocean_gain": jnp.clip(1.0 + 0.1 * jax.random.normal(key_list[11], (OC,), jnp.float32), 0.5, 1.5),
        "ocean_up": normal_values(key_list[12], (OC, OH), OC ** -0.5, 0.375),
        "ocean_down": normal_values(key_list[13], (OH, OC), (OH // 9) ** -0.5, 0.5),
        "surface_weight": normal_values(key_list[14], (OC, FL), OC ** -0.5, 0.375),
        "intersection_point": draw_intersection_point(jax.random.fold_in(key_list[19], 71), 0),
        "intersection_weight": jnp.clip(jnp.exp(math.log(1.0) - 2.3025851 * jax.random.uniform(key_list[16], (ONR, ONC, KOV), jnp.float32) ** steps_of(key_list[16], (ONR, ONC, KOV), ((0, 8), (1, 32)), -0.2, 0.2)), 0.1, 1.0),
        "return_intersection": jnp.clip(jnp.exp(math.log(1.0) - 2.3025851 * jax.random.uniform(key_list[17], (ONR, ONC, KOV), jnp.float32) ** steps_of(key_list[17], (ONR, ONC, KOV), ((0, 8), (1, 32)), -0.2, 0.2)), 0.1, 1.0),
        "ocean_cot": normal_values(key_list[18], (ONR, ONC, OC), 0.01, 0.15625, ((0, 8), (1, 32))),
    }


def dft_forward(lon_total, wave_total):
    longitude = jnp.arange(lon_total, dtype=jnp.int32)[:, None]
    wavenum = jnp.arange(wave_total, dtype=jnp.int32)[None, :]
    phases = (longitude * wavenum % lon_total).astype(jnp.float32) * (2.0 * math.pi / lon_total)
    real_part = jnp.cos(phases) / lon_total
    imag_part = -jnp.sin(phases) / lon_total
    return jnp.stack([real_part, imag_part], axis=-1).reshape(lon_total, 2 * wave_total).astype(jnp.bfloat16)

def dft_inverse(wave_total, lon_total):
    wavenum = jnp.arange(wave_total, dtype=jnp.int32)[:, None]
    longitude = jnp.arange(lon_total, dtype=jnp.int32)[None, :]
    phases = (longitude * wavenum % lon_total).astype(jnp.float32) * (2.0 * math.pi / lon_total)
    factor = jnp.where(wavenum == 0, 1.0, 2.0)
    real_part = factor * jnp.cos(phases)
    imag_part = -factor * jnp.sin(phases)
    return jnp.stack([real_part, imag_part], axis=1).reshape(2 * wave_total, lon_total).astype(jnp.bfloat16)

def quad_weights(lat_total):
    colatitude = math.pi * (jnp.arange(lat_total, dtype=jnp.float32) + 0.5) / lat_total
    return 2.0 * math.pi * (math.pi / lat_total) * jnp.sin(colatitude)

def legendre(orders, lat_total, degrees):
    colatitude = math.pi * (jnp.arange(lat_total, dtype=jnp.float32) + 0.5) / lat_total
    cosine = jnp.cos(colatitude)
    sine_vals = jnp.sin(colatitude)
    order_f = orders.astype(jnp.float32)[:, None]
    counter = jnp.arange(1, degrees, dtype=jnp.float32)[None, :]
    halves = jnp.log((2.0 * counter - 1.0) / (2.0 * counter))
    partial_log = lax.optimization_barrier(jnp.sum(jnp.where(counter <= order_f, halves, 0.0), axis=1, keepdims=True))
    log_start = 0.5 * jnp.log((2.0 * order_f + 1.0) / (4.0 * math.pi)) + 0.5 * partial_log + order_f * jnp.log(sine_vals)[None, :]
    cos_b = cosine[None, :]
    first_step = jnp.sqrt(2.0 * order_f + 3.0) * cos_b

    def block(carry, block_id):
        older, newer = carry
        rows_out = []
        for step in range(32):
            degree_f = (block_id * 32 + step).astype(jnp.float32)
            active = degree_f >= order_f + 2.0
            coef_a = jnp.sqrt(jnp.where(active, 4.0 * degree_f * degree_f - 1.0, 1.0) / jnp.where(active, degree_f * degree_f - order_f * order_f, 1.0))
            coef_b = jnp.sqrt(jnp.where(active, (degree_f - 1.0) * (degree_f - 1.0) - order_f * order_f, 0.0) / jnp.where(active, 4.0 * (degree_f - 1.0) * (degree_f - 1.0) - 1.0, 1.0))
            recurred = coef_a * (cos_b * newer - coef_b * older)
            start_vals = jnp.where(degree_f == order_f + 1.0, first_step, jnp.where(degree_f == order_f, 1.0, 0.0))
            value = jnp.where(active, recurred, start_vals)
            older, newer = (newer, value)
            rows_out.append(value)
        return ((older, newer), jnp.stack(rows_out))
    zeros_init = jnp.zeros((orders.shape[0], lat_total), jnp.float32)
    carry_out, stacked = lax.scan(block, (zeros_init, zeros_init), jnp.arange(degrees // 32, dtype=jnp.int32))
    ratios = stacked.reshape(degrees, orders.shape[0], lat_total)
    values = ratios * jnp.exp(log_start)[None]
    values = jnp.where(log_start[None] > -70.0, values, 0.0)
    return jnp.transpose(values, (1, 0, 2))

def complex_matrix(weights):
    real_part = weights[0]
    imag_part = weights[1]
    upper_half = jnp.concatenate([real_part, imag_part], axis=1)
    lower_half = jnp.concatenate([-imag_part, real_part], axis=1)
    return jnp.concatenate([upper_half, lower_half], axis=0)

def depthwise(padded, kernel, height, breadth):
    running = jnp.zeros((height, breadth, kernel.shape[2]), jnp.float32)
    for row_off in range(7):
        for col_off in range(7):
            running = running + padded[row_off:row_off + height, col_off:col_off + breadth].astype(jnp.float32) * kernel[row_off, col_off].astype(jnp.float32)
    return running

def layer_norm(values, gain):
    mean_val = lax.optimization_barrier(jnp.mean(values, axis=-1, keepdims=True))
    centred = values - mean_val
    variance = lax.optimization_barrier(jnp.mean(centred * centred, axis=-1, keepdims=True))
    return (centred * lax.rsqrt(variance + 1e-06) * gain).astype(jnp.bfloat16)

def reference(atm_state, atm_gain, spec_weight, mlp_in, mlp_out, flux_weight, return_weight, ocean_state, wet, ocean_in, depth_kernel, ocean_gain, ocean_up, ocean_down, surface_weight, intersection_point, intersection_weight, return_intersection, ocean_cot):
    lat_block = 16
    block_count = NLAT // lat_block
    forward_table = dft_forward(NLON, MW)
    inverse_table = dft_inverse(MW, NLON)

    def to_waves(lat_piece):
        state_f = lat_piece.astype(jnp.float32)
        normed = (state_f * lax.rsqrt(lax.optimization_barrier(jnp.mean(state_f * state_f, axis=-1, keepdims=True)) + 1e-06) * atm_gain).astype(jnp.bfloat16)
        return jnp.einsum('alc,lk->akc', normed.astype(jnp.float32), forward_table.astype(jnp.float32)).astype(jnp.bfloat16)
    wave_rows = lax.map(to_waves, atm_state.reshape(block_count, lat_block, NLON, C)).reshape(NLAT, MW, 2 * C)
    mixer = complex_matrix(spec_weight)
    quadrature = quad_weights(NLAT)

    def by_group(group_id):
        orders = group_id * 8 + jnp.arange(8, dtype=jnp.int32)
        legendre_tab = legendre(orders, NLAT, MW)
        analysis = (legendre_tab * quadrature).astype(jnp.bfloat16)
        synthesis = legendre_tab.astype(jnp.bfloat16)
        spectra_in = lax.dynamic_slice_in_dim(wave_rows, (group_id * 8).astype(jnp.int32), 8, 1)
        coeffs = jnp.einsum('mlj,jmx->lmx', analysis.astype(jnp.float32), spectra_in.astype(jnp.float32)).astype(jnp.bfloat16)
        mixed_coef = jnp.dot(coeffs.reshape(MW * 8, 2 * C), mixer, preferred_element_type=jnp.float32).astype(jnp.bfloat16).reshape(MW, 8, 2 * C)
        return jnp.einsum('mlj,lmx->jmx', synthesis.astype(jnp.float32), mixed_coef.astype(jnp.float32)).astype(jnp.bfloat16)
    grid_waves = lax.map(by_group, jnp.arange(MW // 8, dtype=jnp.int32))
    grid_waves = jnp.transpose(grid_waves, (1, 0, 2, 3)).reshape(NLAT, 2 * MW, C)

    def to_grid(lat_piece):
        return jnp.einsum('akc,kl->alc', lat_piece.astype(jnp.float32), inverse_table.astype(jnp.float32)).astype(jnp.bfloat16)
    spectral = lax.map(to_grid, grid_waves.reshape(block_count, lat_block, 2 * MW, C))
    flux_rows = jnp.dot(atm_state.reshape(NLAT * NLON, C), flux_weight, preferred_element_type=jnp.float32).astype(jnp.bfloat16)
    block_cells = LAT_DEV * LON_DEV
    tile_row = (jnp.arange(ONR, dtype=jnp.int32) // ORW)[:, None, None]
    tile_col = (jnp.arange(ONC, dtype=jnp.int32) // OCL)[None, :, None]
    east_flag = (intersection_point >= block_cells).astype(jnp.int32)
    local_ids = intersection_point - east_flag * block_cells
    point_ids = (tile_row * LAT_DEV + local_ids // LON_DEV) * NLON + (tile_col + east_flag) % N_LON * LON_DEV + local_ids % LON_DEV
    forcing = jnp.zeros((ONR, ONC, FL), jnp.float32)
    for intersection in range(KOV):
        picked = jnp.take(flux_rows, point_ids[:, :, intersection].reshape(-1), axis=0).reshape(ONR, ONC, FL)
        forcing = forcing + intersection_weight[:, :, intersection, None] * picked.astype(jnp.float32)
    forcing = forcing.astype(jnp.bfloat16)
    wet_f = wet.astype(jnp.float32)[..., None]
    ocean_mix = ((ocean_state.astype(jnp.float32) + jnp.dot(forcing.reshape(ONR * ONC, FL), ocean_in, preferred_element_type=jnp.float32).reshape(ONR, ONC, OC)) * wet_f).astype(jnp.bfloat16)
    side_ext = jnp.concatenate([ocean_mix[:, ONC - 3:], ocean_mix, ocean_mix[:, :3]], axis=1)
    columns = (jnp.arange(ONC + 6, dtype=jnp.int32) - 3) % ONC
    folded = jnp.take(ocean_mix[ONR - 3:][::-1], ONC - 1 - columns, axis=1)
    padded = jnp.concatenate([jnp.zeros((3, ONC + 6, OC), jnp.bfloat16), side_ext, folded], axis=0)
    depth_sum = depthwise(padded, depth_kernel, ONR, ONC)
    normal = layer_norm(depth_sum, ocean_gain).reshape(ONR * ONC, OC)
    pre = jnp.dot(normal, ocean_up, preferred_element_type=jnp.float32)
    lifted = jax.nn.gelu(pre).astype(jnp.bfloat16)
    ocean_next = ((ocean_mix.astype(jnp.float32) + jnp.dot(lifted, ocean_down, preferred_element_type=jnp.float32).reshape(ONR, ONC, OC)) * wet_f).astype(jnp.bfloat16)
    masked_cot = (ocean_cot.astype(jnp.float32) * wet_f).astype(jnp.bfloat16).reshape(ONR * ONC, OC)
    grad_down = lax.dot_general(lifted, masked_cot, (((0,), (0,)), ((), ())), preferred_element_type=jnp.float32)
    back_hidden = lax.dot_general(masked_cot, ocean_down, (((1,), (1,)), ((), ())), preferred_element_type=jnp.float32)
    gelu_out, pullback = jax.vjp(jax.nn.gelu, pre)
    pre_grad = pullback(back_hidden)[0].astype(jnp.bfloat16)
    grad_up = lax.dot_general(normal, pre_grad, (((0,), (0,)), ((), ())), preferred_element_type=jnp.float32)
    surface = (jnp.dot(ocean_state.reshape(ONR * ONC, OC), surface_weight, preferred_element_type=jnp.float32) * wet.astype(jnp.float32).reshape(ONR * ONC, 1)).astype(jnp.bfloat16)
    surface_f = surface.astype(jnp.float32)
    total_points = NLAT * NLON
    own_sum = jnp.zeros((total_points + 1, FL), jnp.float32)
    east_sum = jnp.zeros((total_points + 1, FL), jnp.float32)
    for intersection in range(KOV):
        ids = point_ids[:, :, intersection].reshape(-1)
        flags = east_flag[:, :, intersection].reshape(-1)
        terms = return_intersection[:, :, intersection].reshape(-1, 1) * surface_f
        own_sum = own_sum + jax.ops.segment_sum(terms, jnp.where(flags == 0, ids, total_points), num_segments=total_points + 1)
        east_sum = east_sum + jax.ops.segment_sum(terms, jnp.where(flags == 1, ids, total_points), num_segments=total_points + 1)
    own_part = lax.optimization_barrier(own_sum[:total_points].astype(jnp.bfloat16))
    east_part = lax.optimization_barrier(east_sum[:total_points].astype(jnp.bfloat16))
    returned = (own_part.astype(jnp.float32) + east_part.astype(jnp.float32)).astype(jnp.bfloat16)

    def finish(pieces):
        state_piece, spec_piece, ret_piece = pieces
        hidden = (state_piece.astype(jnp.float32) + spec_piece.astype(jnp.float32)).astype(jnp.bfloat16).reshape(lat_block * NLON, C)
        activation = jax.nn.gelu(jnp.dot(hidden, mlp_in, preferred_element_type=jnp.float32)).astype(jnp.bfloat16)
        result = hidden.astype(jnp.float32) + jnp.dot(activation, mlp_out, preferred_element_type=jnp.float32) + jnp.dot(ret_piece, return_weight, preferred_element_type=jnp.float32)
        return result.astype(jnp.bfloat16).reshape(lat_block, NLON, C)
    atm_next = lax.map(finish, (atm_state.reshape(block_count, lat_block, NLON, C), spectral, returned.reshape(block_count, lat_block * NLON, FL))).reshape(NLAT, NLON, C)
    return (atm_next, ocean_next, grad_up, grad_down)
```

```python
import functools
import math

import jax
import jax.numpy as jnp
import ml_dtypes
import numpy as np
from jax import lax
from jax.experimental import pallas as pl
from jax.experimental.pallas import tpu as pltpu
from jax.sharding import Mesh
from jax.sharding import PartitionSpec as P

C = 384
HID = 768
NLAT = 512
NLON = 1024
MW = 512
FL = 128
OC = 256
OH = 1024
ROWS = 64
COLS = 32
POINTS = ROWS * COLS
EAST = ROWS * 16
CELLS = 256
KOV = 4
DEV = 256
BF = jnp.bfloat16
F32 = jnp.float32
GELU_K = math.sqrt(2.0 / math.pi)

NN = (((1,), (0,)), ((), ()))
NT = (((1,), (1,)), ((), ()))
TN = (((0,), (0,)), ((), ()))


def dot(a, b, dims=NN):
    return lax.dot_general(a, b, dims, preferred_element_type=F32)


def orders_of_device():
    d = np.arange(DEV)
    return np.stack([d, MW - 1 - d], axis=1)


@functools.cache
def dft_tables():
    orders = orders_of_device().T
    lon = np.arange(NLON)
    phase = 2.0 * np.pi * ((orders[:, :, None] * lon) % NLON) / NLON
    forward = np.stack([np.cos(phase), -np.sin(phase)], axis=1) / NLON
    factor = np.where(orders == 0, 1.0, 2.0)[:, None, :, None]
    inverse = np.stack([np.cos(phase), -np.sin(phase)], axis=1) * factor
    forward = forward.reshape(2 * MW, NLON).astype(np.float32).astype(ml_dtypes.bfloat16)
    inverse = inverse.reshape(2 * MW, NLON).T.astype(np.float32).astype(ml_dtypes.bfloat16)
    return forward, np.ascontiguousarray(inverse)


@functools.cache
def legendre_constants():
    orders = orders_of_device().astype(np.float64)
    lat = np.concatenate([np.arange(0, NLAT, 2), np.arange(1, NLAT, 2)])
    theta = np.pi * (lat + 0.5) / NLAT
    k = np.arange(1, MW, dtype=np.float64)
    partial = np.concatenate([[0.0], np.cumsum(np.log((2 * k - 1) / (2 * k)))])
    partial = partial[orders_of_device()]
    log_s = (0.5 * np.log((2 * orders + 1) / (4 * np.pi)) + 0.5 * partial)[:, :, None]
    log_s = log_s + orders[:, :, None] * np.log(np.sin(theta))
    seed = np.where(log_s > -70.0, np.exp(log_s), 0.0).astype(np.float32)
    seed = seed.reshape(DEV, 8, 128)
    cosine = np.tile(np.cos(theta).astype(np.float32).reshape(4, 128), (2, 1))
    quad = (2.0 * np.pi * (np.pi / NLAT) * np.sin(theta)).astype(np.float32).reshape(4, 128)
    degree = np.arange(MW, dtype=np.float64)
    m = orders[:, :, None]
    live = degree >= m + 1
    a = np.sqrt((4 * degree**2 - 1) / np.where(live, degree**2 - m**2, 1.0), where=live, out=np.zeros(live.shape))
    b2 = np.where(live, (degree - 1) ** 2 - m**2, 0.0) / np.where(live, 4 * (degree - 1) ** 2 - 1, 1.0)
    b = np.sqrt(np.maximum(b2, 0.0))
    coef = np.concatenate([a, a * b], axis=1).astype(np.float32)
    return seed, cosine, quad, coef


def legendre_kernel(dev_ref, coef_ref, seed_ref, cos_ref, quad_ref, ana_ref, syn_ref, vals):
    dev = dev_ref[0]
    upper = lax.broadcasted_iota(jnp.int32, (8, 128), 0) < 4
    order = jnp.where(upper, dev, MW - 1 - dev)
    seed = seed_ref[0]
    cosine = cos_ref[...]

    def block(i, carry):
        older, newer = carry
        for step in range(16):
            l = i * 16 + step
            a = jnp.where(upper, coef_ref[0, 0, l], coef_ref[0, 1, l]) * cosine
            ab = jnp.where(upper, coef_ref[0, 2, l], coef_ref[0, 3, l])
            value = a * newer - ab * older
            value = jnp.where(order == l, seed, value)
            vals[pl.ds(pl.multiple_of(l * 8, 8), 8), :] = value
            older, newer = newer, value
        return older, newer

    zero = jnp.zeros((8, 128), F32)
    lax.fori_loop(0, MW // 16, block, (zero, zero))
    for m in range(2):
        for jc in range(4):
            table = vals[pl.ds(m * 4 + jc, MW, stride=8), :]
            ana_ref[m, :, jc * 128 : (jc + 1) * 128] = (table * quad_ref[jc : jc + 1, :]).astype(BF)
            syn_ref[m, :, jc * 128 : (jc + 1) * 128] = table.astype(BF)


def legendre_tables(dev):
    seed, cosine, quad, coef = legendre_constants()
    table = jax.ShapeDtypeStruct((2, MW, NLAT), BF)
    whole = lambda *shape: pl.BlockSpec(shape, lambda i, d: (0,) * len(shape))
    return pl.pallas_call(
        legendre_kernel,
        out_shape=(table, table),
        grid_spec=pltpu.PrefetchScalarGridSpec(
            num_scalar_prefetch=1,
            grid=(1,),
            in_specs=[
                pl.BlockSpec((1, 4, MW), lambda i, d: (d[0], 0, 0), memory_space=pltpu.SMEM),
                pl.BlockSpec((1, 8, 128), lambda i, d: (d[0], 0, 0)),
                whole(8, 128),
                whole(4, 128),
            ],
            out_specs=[whole(2, MW, NLAT), whole(2, MW, NLAT)],
            scratch_shapes=[pltpu.VMEM((MW * 8, 128), F32)],
        ),
        compiler_params=pltpu.CompilerParams(vmem_limit_bytes=32 << 20),
        cost_estimate=pl.CostEstimate(flops=10_000_000, bytes_accessed=4_000_000, transcendentals=0),
        name="legendre",
    )(dev, jnp.asarray(coef), jnp.asarray(seed), jnp.asarray(cosine), jnp.asarray(quad))


def norm_kernel(x_ref, gain_ref, fw_ref, msg_ref, flux_ref, west_ref):
    x = x_ref[...]
    xf = x.astype(F32)
    scale = lax.rsqrt(jnp.mean(xf * xf, axis=-1, keepdims=True) + 1e-06)
    normed = (xf * scale * gain_ref[...].reshape(1, 1, C)).astype(BF)
    pairs = normed.reshape(x.shape[0] // 2, 2, COLS, C)
    msg_ref[:, :, :C] = pairs[:, 0]
    msg_ref[:, :, C:] = pairs[:, 1]
    flux = dot(x.reshape(-1, C), fw_ref[...]).astype(BF)
    flux_ref[...] = flux
    west_ref[...] = flux.reshape(x.shape[0], 2, 16, FL)[:, 0].reshape(-1, FL)


def norm_and_flux(atm_state, gain, flux_weight):
    step = 16
    return pl.pallas_call(
        norm_kernel,
        grid=(ROWS // step,),
        out_shape=(
            jax.ShapeDtypeStruct((ROWS // 2, COLS, 2 * C), BF),
            jax.ShapeDtypeStruct((POINTS, FL), BF),
            jax.ShapeDtypeStruct((EAST, FL), BF),
        ),
        in_specs=[
            pl.BlockSpec((step, COLS, C), lambda i: (i, 0, 0)),
            pl.BlockSpec((1, C), lambda i: (0, 0)),
            pl.BlockSpec((C, FL), lambda i: (0, 0)),
        ],
        out_specs=[
            pl.BlockSpec((step // 2, COLS, 2 * C), lambda i: (i, 0, 0)),
            pl.BlockSpec((step * COLS, FL), lambda i: (i, 0)),
            pl.BlockSpec((step * 16, FL), lambda i: (i, 0)),
        ],
        compiler_params=pltpu.CompilerParams(vmem_limit_bytes=32 << 20),
        cost_estimate=pl.CostEstimate(flops=210_000_000, bytes_accessed=4_000_000, transcendentals=0),
        name="norm_flux",
    )(atm_state, gain.reshape(1, C), flux_weight)


def interleave(acc, matrix, mp):
    for a in range(2):
        for t in range(3):
            lane = a * C + t * 128
            acc[t, pl.ds(a * 4 + mp, DEV, stride=8), :] = matrix[:, lane : lane + 128]


def drain(acc, out_ref):
    for t in range(3):
        out_ref[:, :, t * 128 : (t + 1) * 128] = acc[t].reshape(DEV, 8, 128).astype(BF)


def fill(acc, in_ref):
    for t in range(3):
        acc[t] = in_ref[:, :, t * 128 : (t + 1) * 128].astype(F32).reshape(DEV * 8, 128)


def picked(acc, a, mp, t):
    return acc[t, pl.ds(a * 4 + mp, DEV, stride=8), :].astype(BF)


def dft_kernel(x_ref, table_ref, out_ref, acc):
    x = x_ref[...].reshape(NLON, 2 * C)
    for part in range(4):
        res = dot(table_ref[part * DEV : (part + 1) * DEV, :], x)
        interleave(acc, res, part)
    drain(acc, out_ref)


def dft(rows, table):
    return pl.pallas_call(
        dft_kernel,
        out_shape=jax.ShapeDtypeStruct((DEV, 8, C), BF),
        scratch_shapes=[pltpu.VMEM((3, DEV * 8, 128), F32)],
        compiler_params=pltpu.CompilerParams(vmem_limit_bytes=32 << 20),
        cost_estimate=pl.CostEstimate(flops=1_700_000_000, bytes_accessed=6_000_000, transcendentals=0),
        name="dft",
    )(rows, table)


def inverse_kernel(w_ref, table_ref, out_ref, acc, waves):
    fill(acc, w_ref)
    for part in range(4):
        for a in range(2):
            for t in range(3):
                lane = a * C + t * 128
                waves[part * DEV : (part + 1) * DEV, lane : lane + 128] = picked(acc, a, part, t)
    for t in range(4):
        res = dot(table_ref[t * 256 : (t + 1) * 256, :], waves[...])
        out_ref[t * 8 : (t + 1) * 8] = res.astype(BF).reshape(8, COLS, 2 * C)


def inverse_dft(waves, table):
    return pl.pallas_call(
        inverse_kernel,
        out_shape=jax.ShapeDtypeStruct((32, COLS, 2 * C), BF),
        scratch_shapes=[pltpu.VMEM((3, DEV * 8, 128), F32), pltpu.VMEM((2 * MW, 2 * C), BF)],
        compiler_params=pltpu.CompilerParams(vmem_limit_bytes=32 << 20),
        cost_estimate=pl.CostEstimate(flops=1_700_000_000, bytes_accessed=6_000_000, transcendentals=0),
        name="inverse_dft",
    )(waves, table)


def spectral_kernel(w_ref, ana_ref, syn_ref, sw_ref, out_ref, acc, waves, mixer):
    mixer[:C, :C] = sw_ref[0]
    mixer[:C, C:] = sw_ref[1]
    mixer[C:, :C] = -sw_ref[1]
    mixer[C:, C:] = sw_ref[0]
    fill(acc, w_ref)
    for m in range(2):
        for p in range(2):
            for a in range(2):
                for t in range(3):
                    lane = p * C + t * 128
                    waves[a * DEV : (a + 1) * DEV, lane : lane + 128] = picked(acc, a, m * 2 + p, t)
        coeff = dot(ana_ref[m], waves[...]).astype(BF)
        mixed = dot(coeff, mixer[...]).astype(BF)
        grid = dot(syn_ref[m], mixed, TN)
        for p in range(2):
            for a in range(2):
                for t in range(3):
                    lane = p * C + t * 128
                    acc[t, pl.ds(a * 4 + m * 2 + p, DEV, stride=8), :] = grid[
                        a * DEV : (a + 1) * DEV, lane : lane + 128
                    ]
    drain(acc, out_ref)


def spectral_mix(waves, analysis, synthesis, spec_weight):
    return pl.pallas_call(
        spectral_kernel,
        out_shape=jax.ShapeDtypeStruct((DEV, 8, C), BF),
        scratch_shapes=[
            pltpu.VMEM((3, DEV * 8, 128), F32),
            pltpu.VMEM((NLAT, 2 * C), BF),
            pltpu.VMEM((2 * C, 2 * C), BF),
        ],
        compiler_params=pltpu.CompilerParams(vmem_limit_bytes=40 << 20),
        cost_estimate=pl.CostEstimate(flops=2_900_000_000, bytes_accessed=6_000_000, transcendentals=0),
        name="spectral_mix",
    )(waves, analysis, synthesis, spec_weight)


def gelu_parts(x):
    t = jnp.tanh(GELU_K * (x + 0.044715 * (x * x * x)))
    return 0.5 * (1.0 + t), t


def finish_kernel(x_ref, s_ref, own_ref, west_ref, w1_ref, w2_ref, rw_ref, out_ref):
    rows = x_ref.shape[0]
    x = x_ref[...].astype(F32).reshape(rows // 2, 2, COLS, C)
    hidden = jnp.stack(
        [x[:, 0] + s_ref[:, :, :C].astype(F32), x[:, 1] + s_ref[:, :, C:].astype(F32)], axis=1
    )
    hidden = hidden.reshape(rows * COLS, C).astype(BF)
    pre = dot(hidden, w1_ref[...])
    act = (pre * gelu_parts(pre)[0]).astype(BF)
    own = own_ref[...].astype(F32).reshape(rows, 2, 16, FL)
    west = own[:, 0] + west_ref[...].astype(F32).reshape(rows, 16, FL)
    returned = jnp.stack([west, own[:, 1]], axis=1).reshape(rows * COLS, FL).astype(BF)
    out = hidden.astype(F32) + dot(act, w2_ref[...]) + dot(returned, rw_ref[...])
    out_ref[...] = out.astype(BF).reshape(rows, COLS, C)


def finish(atm_state, spectral, own, west, mlp_in, mlp_out, return_weight):
    step = 16
    return pl.pallas_call(
        finish_kernel,
        grid=(ROWS // step,),
        out_shape=jax.ShapeDtypeStruct((ROWS, COLS, C), BF),
        in_specs=[
            pl.BlockSpec((step, COLS, C), lambda i: (i, 0, 0)),
            pl.BlockSpec((step // 2, COLS, 2 * C), lambda i: (i, 0, 0)),
            pl.BlockSpec((step * COLS, FL), lambda i: (i, 0)),
            pl.BlockSpec((step * 16, FL), lambda i: (i, 0)),
            pl.BlockSpec((C, HID), lambda i: (0, 0)),
            pl.BlockSpec((HID, C), lambda i: (0, 0)),
            pl.BlockSpec((FL, C), lambda i: (0, 0)),
        ],
        out_specs=pl.BlockSpec((step, COLS, C), lambda i: (i, 0, 0)),
        compiler_params=pltpu.CompilerParams(vmem_limit_bytes=40 << 20),
        cost_estimate=pl.CostEstimate(flops=2_700_000_000, bytes_accessed=6_000_000, transcendentals=1_600_000),
        name="finish",
    )(atm_state, spectral, own, west, mlp_in, mlp_out, return_weight)


def scatter_kernel(state_ref, sw_ref, wet_ref, point_ref, weight_ref, own_ref, east_ref):
    surface = (dot(state_ref[...].reshape(CELLS, OC), sw_ref[...]) * wet_ref[...]).astype(BF)

    def spread(first, count):
        ids = first + lax.broadcasted_iota(jnp.int32, (count, CELLS), 0)
        total = jnp.zeros((count, CELLS), F32)
        for k in range(KOV):
            total = total + jnp.where(ids == point_ref[k : k + 1, :], weight_ref[k : k + 1, :], 0.0)
        return dot(total.astype(BF), surface).astype(BF)

    for i in range(4):
        own_ref[i * 512 : (i + 1) * 512, :] = spread(i * 512, 512)
    for i in range(2):
        east_ref[i * 512 : (i + 1) * 512, :] = spread(POINTS + i * 512, 512)


def scatter(ocean_state, surface_weight, wet_col, points, weights):
    return pl.pallas_call(
        scatter_kernel,
        out_shape=(
            jax.ShapeDtypeStruct((POINTS, FL), BF),
            jax.ShapeDtypeStruct((EAST, FL), BF),
        ),
        compiler_params=pltpu.CompilerParams(vmem_limit_bytes=32 << 20),
        cost_estimate=pl.CostEstimate(flops=250_000_000, bytes_accessed=1_500_000, transcendentals=0),
        name="scatter",
    )(ocean_state, surface_weight, wet_col, points, weights)


def gather_kernel(flux_ref, east_ref, state_ref, wet_ref, oin_ref, point_ref, weight_ref, out_ref):
    def pick(first, count, source):
        ids = first + lax.broadcasted_iota(jnp.int32, (CELLS, count), 1)
        total = jnp.zeros((CELLS, count), F32)
        for k in range(KOV):
            total = total + jnp.where(ids == point_ref[:, k : k + 1], weight_ref[:, k : k + 1], 0.0)
        return dot(total.astype(BF), source)

    forcing = jnp.zeros((CELLS, FL), F32)
    for i in range(4):
        forcing = forcing + pick(i * 512, 512, flux_ref[i * 512 : (i + 1) * 512, :])
    for i in range(2):
        forcing = forcing + pick(POINTS + i * 512, 512, east_ref[i * 512 : (i + 1) * 512, :])
    added = dot(forcing.astype(BF), oin_ref[...])
    state = state_ref[...].reshape(CELLS, OC).astype(F32)
    out_ref[...] = ((state + added) * wet_ref[...]).astype(BF).reshape(16, 16, OC)


def gather(flux, east, ocean_state, wet_col, ocean_in, points, weights):
    return pl.pallas_call(
        gather_kernel,
        out_shape=jax.ShapeDtypeStruct((16, 16, OC), BF),
        compiler_params=pltpu.CompilerParams(vmem_limit_bytes=32 << 20),
        cost_estimate=pl.CostEstimate(flops=250_000_000, bytes_accessed=1_500_000, transcendentals=0),
        name="gather",
    )(flux, east, ocean_state, wet_col, ocean_in, points, weights)


def ocean_kernel(
    mix_ref, west_ref, east_ref, south_ref, north_ref, dk_ref, gain_ref, up_ref, down_ref, wet_ref, cot_ref,
    next_ref, grad_ref, pad,
):
    pad[0:3] = south_ref[...].astype(F32)
    pad[3:19, 0:3] = west_ref[...].astype(F32)
    pad[3:19, 3:19] = mix_ref[...].astype(F32)
    pad[3:19, 19:22] = east_ref[...].astype(F32)
    pad[19:22] = north_ref[...].astype(F32)
    depth = jnp.zeros((16, 16, OC), F32)
    for j in range(7):
        shifted = pad[:, j : j + 16, :]
        for i in range(7):
            depth = depth + shifted[i : i + 16] * dk_ref[i * 7 + j : i * 7 + j + 1, :].astype(F32).reshape(1, 1, OC)
    depth = depth.reshape(CELLS, OC)
    centred = depth - jnp.mean(depth, axis=-1, keepdims=True)
    variance = jnp.mean(centred * centred, axis=-1, keepdims=True)
    normal = (centred * lax.rsqrt(variance + 1e-06) * gain_ref[...]).astype(BF)
    wet = wet_ref[...]
    cot = (cot_ref[...].reshape(CELLS, OC).astype(F32) * wet).astype(BF)
    total = jnp.zeros((CELLS, OC), F32)
    for h in range(4):
        cut = slice(h * 256, (h + 1) * 256)
        pre = dot(normal, up_ref[:, cut])
        half, t = gelu_parts(pre)
        lifted = (pre * half).astype(BF)
        total = total + dot(lifted, down_ref[cut, :])
        gdown = dot(lifted, cot, TN).astype(BF)
        grad_ref[h * 8 : (h + 1) * 8, 32:, :] = gdown.reshape(8, 32, OC)
        slope = half + 0.5 * pre * (1.0 - t * t) * (GELU_K * (1.0 + 3.0 * 0.044715 * (pre * pre)))
        pre_grad = (dot(cot, down_ref[cut, :], NT) * slope).astype(BF)
        gup = dot(normal, pre_grad, TN).astype(BF)
        grad_ref[:, h * 8 : (h + 1) * 8, :] = gup.reshape(32, 8, 256)
    mix = mix_ref[...].reshape(CELLS, OC).astype(F32)
    next_ref[...] = ((mix + total) * wet).astype(BF).reshape(16, 16, OC)


def ocean(mix, west, east, south, north, depth_kernel, gain, up, down, wet_col, cot):
    return pl.pallas_call(
        ocean_kernel,
        out_shape=(
            jax.ShapeDtypeStruct((16, 16, OC), BF),
            jax.ShapeDtypeStruct((32, 64, 256), BF),
        ),
        scratch_shapes=[pltpu.VMEM((22, 22, OC), F32)],
        compiler_params=pltpu.CompilerParams(vmem_limit_bytes=40 << 20),
        cost_estimate=pl.CostEstimate(flops=700_000_000, bytes_accessed=4_000_000, transcendentals=260_000),
        name="ocean",
    )(mix, west, east, south, north, depth_kernel.reshape(49, OC), gain.reshape(1, OC), up, down, wet_col, cot)


def sum_kernel(parts_ref, out_ref):
    total = parts_ref[0].astype(F32)
    for i in range(1, parts_ref.shape[0]):
        total = total + parts_ref[i].astype(F32)
    out_ref[...] = total.astype(BF)


def sum_parts(parts, name):
    return pl.pallas_call(
        sum_kernel,
        out_shape=jax.ShapeDtypeStruct(parts.shape[1:], BF),
        cost_estimate=pl.CostEstimate(flops=parts.size, bytes_accessed=parts.size * 2, transcendentals=0),
        name=name,
    )(parts)


def unpack_kernel(parts_ref, up_ref, down_ref):
    for q in range(4):
        block = parts_ref[:, q * 8 : (q + 1) * 8, :].astype(F32)
        up_ref[:, q * 256 : (q + 1) * 256] = block.reshape(256, 256)
    down_ref[...] = parts_ref[:, 32:, :].astype(F32).reshape(OH, OC)


def unpack(parts):
    return pl.pallas_call(
        unpack_kernel,
        out_shape=(jax.ShapeDtypeStruct((OC, OH), F32), jax.ShapeDtypeStruct((OH, OC), F32)),
        cost_estimate=pl.CostEstimate(flops=1_000_000, bytes_accessed=3_000_000, transcendentals=0),
        name="unpack",
    )(parts)


def exchange(x, axes):
    return lax.all_to_all(x, axes, split_axis=0, concat_axis=0, tiled=True)


def spread(x, axes, count):
    return exchange(jnp.broadcast_to(x[None], (count, *x.shape)), axes)


def after(x, *others):
    return lax.optimization_barrier((x, *others))[0]


def ring(count, distance):
    return [(i, (i + distance) % count) for i in range(count)]


def local(
    atm_state,
    atm_gain,
    spec_weight,
    mlp_in,
    mlp_out,
    flux_weight,
    return_weight,
    ocean_state,
    wet,
    ocean_in,
    depth_kernel,
    ocean_gain,
    ocean_up,
    ocean_down,
    surface_weight,
    intersection_point,
    intersection_weight,
    return_intersection,
    ocean_cot,
):
    lat = lax.axis_index(LAT)
    lon = lax.axis_index(LON)
    dev = (lat * 32 + lon).astype(jnp.int32).reshape(1)
    forward_np, inverse_np = dft_tables()
    forward_table = jnp.asarray(forward_np)
    inverse_table = jnp.asarray(inverse_np)

    msg, flux, flux_west = norm_and_flux(atm_state, atm_gain, flux_weight)
    rows = exchange(msg, LON)

    flux_east = lax.ppermute(flux_west, LON, ring(32, -1))
    away = intersection_point - POINTS
    points = jnp.where(
        away < 0, intersection_point, POINTS + (away // COLS) * 16 + away % COLS
    ).reshape(CELLS, KOV)
    wet_col = wet.astype(F32).reshape(CELLS, 1)
    own, to_east = scatter(
        ocean_state, surface_weight, wet_col, points.T, return_intersection.reshape(CELLS, KOV).T
    )
    analysis, synthesis = legendre_tables(after(dev, msg))
    mix = gather(
        flux, flux_east, ocean_state, wet_col, ocean_in, points, intersection_weight.reshape(CELLS, KOV)
    )
    rows = after(rows, mix, analysis, to_east)

    waves = dft(rows, forward_table)
    by_order = exchange(waves, ALL)

    mix_2, to_east = lax.optimization_barrier((mix, to_east, waves))[:2]
    from_west = lax.ppermute(to_east, LON, ring(32, 1))
    west = lax.ppermute(mix_2[:, 13:], LON, ring(32, 1))
    east = lax.ppermute(mix_2[:, :3], LON, ring(32, -1))
    wide = lambda rows_of: jnp.concatenate(
        [west[rows_of], mix_2[rows_of], east[rows_of]], axis=1
    )
    top = wide(slice(13, 16))
    south = lax.ppermute(top, LAT, [(i, i + 1) for i in range(7)])
    north = lax.ppermute(wide(slice(0, 3)), LAT, [(i + 1, i) for i in range(7)])
    fold = lax.ppermute(top[::-1, ::-1], LON, [(i, 31 - i) for i in range(32)])
    north = jnp.where(lat == 7, fold, north)
    ocean_next, grads = ocean(
        mix_2, west, east, south, north, depth_kernel, ocean_gain, ocean_up, ocean_down, wet_col, ocean_cot
    )
    by_order = after(by_order, grads)

    mixed = spectral_mix(by_order, analysis, synthesis, spec_weight)
    by_row = exchange(mixed, ALL)

    grads = after(grads, mixed)
    plane = sum_parts(exchange(grads, PLANE), "plane_sum")
    column = sum_parts(spread(plane, COLUMN, 8), "column_sum")
    by_row = after(by_row, column)

    grid = inverse_dft(by_row, inverse_table)
    spectral = exchange(grid, LON)

    grad_up, grad_down = unpack(spread(after(column, grid), PLANE, 32))
    spectral = after(spectral, grad_up)

    atm_next = finish(atm_state, spectral, own, from_west, mlp_in, mlp_out, return_weight)
    return (atm_next, ocean_next, grad_up, grad_down)


LAT = ("zh", "core")
LON = ("y", "zl", "x")
ALL = LAT + LON
PLANE = ("core", "y", "x")
COLUMN = ("zh", "zl")


def solution(mesh):
    fine = Mesh(mesh.devices.reshape(4, 2, 4, 2, 4), ALL)
    block = P(LAT, LON)
    whole = P()
    in_specs = (block,) + (whole,) * 6 + (block,) * 2 + (whole,) * 6 + (block,) * 4
    out_specs = (block, block, whole, whole)
    return jax.shard_map(local, mesh=fine, in_specs=in_specs, out_specs=out_specs, check_vma=False)
```

```python
import functools
import math

import jax
import jax.numpy as jnp
import ml_dtypes
import numpy as np
from jax import lax
from jax.experimental import pallas as pl
from jax.experimental.pallas import tpu as pltpu
from jax.sharding import Mesh
from jax.sharding import PartitionSpec as P

C = 384
HID = 768
NLAT = 512
NLON = 1024
MW = 512
FL = 128
OC = 256
OH = 1024
ROWS = 64
COLS = 32
POINTS = ROWS * COLS
EAST = ROWS * 16
CELLS = 256
KOV = 4
DEV = 256
BF = jnp.bfloat16
F32 = jnp.float32
GELU_K = math.sqrt(2.0 / math.pi)

PARAMS = pltpu.CompilerParams(vmem_limit_bytes=56 << 20)

NN = (((1,), (0,)), ((), ()))
NT = (((1,), (1,)), ((), ()))
TN = (((0,), (0,)), ((), ()))


ANY = pl.BlockSpec(memory_space=pl.ANY)


def dot(a, b, dims=NN):
    return lax.dot_general(a, b, dims, preferred_element_type=F32)


def orders_of_device():
    d = np.arange(DEV)
    return np.stack([d, MW - 1 - d], axis=1)


@functools.cache
def dft_tables():
    orders = orders_of_device().T
    lon = np.arange(NLON)
    phase = 2.0 * np.pi * ((orders[:, :, None] * lon) % NLON) / NLON
    forward = np.stack([np.cos(phase), -np.sin(phase)], axis=1) / NLON
    factor = np.where(orders == 0, 1.0, 2.0)[:, None, :, None]
    inverse = np.stack([np.cos(phase), -np.sin(phase)], axis=1) * factor
    forward = forward.reshape(2 * MW, NLON).astype(np.float32).astype(ml_dtypes.bfloat16)
    inverse = inverse.reshape(2 * MW, NLON).T.astype(np.float32).astype(ml_dtypes.bfloat16)
    return forward, np.ascontiguousarray(inverse)


@functools.cache
def legendre_constants():
    orders = orders_of_device().astype(np.float64)
    lat = np.concatenate([np.arange(0, NLAT, 2), np.arange(1, NLAT, 2)])
    theta = np.pi * (lat + 0.5) / NLAT
    k = np.arange(1, MW, dtype=np.float64)
    partial = np.concatenate([[0.0], np.cumsum(np.log((2 * k - 1) / (2 * k)))])
    partial = partial[orders_of_device()]
    log_s = (0.5 * np.log((2 * orders + 1) / (4 * np.pi)) + 0.5 * partial)[:, :, None]
    log_s = log_s + orders[:, :, None] * np.log(np.sin(theta))
    seed = np.where(log_s > -70.0, np.exp(log_s), 0.0).astype(np.float32)
    seed = seed.reshape(DEV, 8, 128)
    cosine = np.tile(np.cos(theta).astype(np.float32).reshape(4, 128), (2, 1))
    quad = (2.0 * np.pi * (np.pi / NLAT) * np.sin(theta)).astype(np.float32).reshape(4, 128)
    degree = np.arange(MW, dtype=np.float64)
    m = orders[:, :, None]
    live = degree >= m + 1
    a = np.sqrt((4 * degree**2 - 1) / np.where(live, degree**2 - m**2, 1.0), where=live, out=np.zeros(live.shape))
    b2 = np.where(live, (degree - 1) ** 2 - m**2, 0.0) / np.where(live, 4 * (degree - 1) ** 2 - 1, 1.0)
    b = np.sqrt(np.maximum(b2, 0.0))
    coef = np.concatenate([a, a * b], axis=1).astype(np.float32)
    return seed, cosine, quad, coef


def legendre_kernel(dev_ref, coef_ref, seed_ref, cos_ref, quad_ref, order_ref, ana_ref, syn_ref, vals):
    dev = dev_ref[0]
    upper = lax.broadcasted_iota(jnp.int32, (8, 128), 0) < 4
    order = jnp.where(upper, dev, MW - 1 - dev)
    seed = seed_ref[0]
    cosine = cos_ref[...]

    def block(i, carry):
        older, newer = carry
        for step in range(16):
            l = i * 16 + step
            a = jnp.where(upper, coef_ref[0, 0, l], coef_ref[0, 1, l]) * cosine
            ab = jnp.where(upper, coef_ref[0, 2, l], coef_ref[0, 3, l])
            value = a * newer - ab * older
            value = jnp.where(order == l, seed, value)
            vals[pl.ds(pl.multiple_of(l * 8, 8), 8), :] = value
            older, newer = newer, value
        return older, newer

    zero = jnp.zeros((8, 128), F32)
    lax.fori_loop(0, MW // 16, block, (zero, zero))
    for m in range(2):
        for jc in range(4):
            table = vals[pl.ds(m * 4 + jc, MW, stride=8), :]
            ana_ref[m, :, jc * 128 : (jc + 1) * 128] = (table * quad_ref[jc : jc + 1, :]).astype(BF)
            syn_ref[m, :, jc * 128 : (jc + 1) * 128] = table.astype(BF)


def legendre_tables(dev, earlier):
    seed, cosine, quad, coef = legendre_constants()
    table = jax.ShapeDtypeStruct((2, MW, NLAT), BF)
    whole = lambda *shape: pl.BlockSpec(shape, lambda i, d: (0,) * len(shape))
    return pl.pallas_call(
        legendre_kernel,
        out_shape=(table, table),
        grid_spec=pltpu.PrefetchScalarGridSpec(
            num_scalar_prefetch=1,
            grid=(1,),
            in_specs=[
                pl.BlockSpec((1, 4, MW), lambda i, d: (d[0], 0, 0), memory_space=pltpu.SMEM),
                pl.BlockSpec((1, 8, 128), lambda i, d: (d[0], 0, 0)),
                whole(8, 128),
                whole(4, 128),
                ANY,
            ],
            out_specs=[whole(2, MW, NLAT), whole(2, MW, NLAT)],
            scratch_shapes=[pltpu.VMEM((MW * 8, 128), F32)],
        ),
        compiler_params=PARAMS,
        cost_estimate=pl.CostEstimate(flops=10_000_000, bytes_accessed=4_000_000, transcendentals=0),
        name="legendre",
    )(dev, jnp.asarray(coef), jnp.asarray(seed), jnp.asarray(cosine), jnp.asarray(quad), earlier)


def flux_kernel(x_ref, fw_ref, flux_ref, west_ref):
    x = x_ref[...]
    flux = dot(x.reshape(-1, C), fw_ref[...]).astype(BF)
    flux_ref[...] = flux
    west_ref[...] = flux.reshape(x.shape[0], 2, 16, FL)[:, 0].reshape(-1, FL)


def surface_flux(atm_state, flux_weight):
    step = 16
    return pl.pallas_call(
        flux_kernel,
        grid=(ROWS // step,),
        out_shape=(
            jax.ShapeDtypeStruct((POINTS, FL), BF),
            jax.ShapeDtypeStruct((EAST, FL), BF),
        ),
        in_specs=[
            pl.BlockSpec((step, COLS, C), lambda i: (i, 0, 0)),
            pl.BlockSpec((C, FL), lambda i: (0, 0)),
        ],
        out_specs=[
            pl.BlockSpec((step * COLS, FL), lambda i: (i, 0)),
            pl.BlockSpec((step * 16, FL), lambda i: (i, 0)),
        ],
        compiler_params=PARAMS,
        cost_estimate=pl.CostEstimate(flops=210_000_000, bytes_accessed=2_500_000, transcendentals=0),
        name="flux",
    )(atm_state, flux_weight)


def norm_kernel(x_ref, gain_ref, order_ref, msg_ref):
    x = x_ref[...]
    xf = x.astype(F32)
    scale = lax.rsqrt(jnp.mean(xf * xf, axis=-1, keepdims=True) + 1e-06)
    normed = (xf * scale * gain_ref[...].reshape(1, 1, C)).astype(BF)
    pairs = normed.reshape(x.shape[0] // 2, 2, COLS, C)
    msg_ref[:, :, :C] = pairs[:, 0]
    msg_ref[:, :, C:] = pairs[:, 1]


def norm(atm_state, gain, earlier):
    step = 16
    return pl.pallas_call(
        norm_kernel,
        grid=(ROWS // step,),
        out_shape=jax.ShapeDtypeStruct((ROWS // 2, COLS, 2 * C), BF),
        in_specs=[
            pl.BlockSpec((step, COLS, C), lambda i: (i, 0, 0)),
            pl.BlockSpec((C,), lambda i: (0,)),
            ANY,
        ],
        out_specs=pl.BlockSpec((step // 2, COLS, 2 * C), lambda i: (i, 0, 0)),
        compiler_params=PARAMS,
        cost_estimate=pl.CostEstimate(flops=10_000_000, bytes_accessed=3_000_000, transcendentals=0),
        name="norm",
    )(atm_state, gain, earlier)


def interleave(acc, matrix, mp):
    for a in range(2):
        for t in range(3):
            lane = a * C + t * 128
            acc[t, pl.ds(a * 4 + mp, DEV, stride=8), :] = matrix[:, lane : lane + 128]


def picked(acc, a, mp, t):
    return acc[t, pl.ds(a * 4 + mp, DEV, stride=8), :].astype(BF)


def pieces(source, target, sems, first):
    rows = source.shape[0] // 4
    return [
        pltpu.make_async_copy(
            source.at[pl.ds(i * rows, rows)], target.at[pl.ds(i * rows, rows)], sems.at[first + i]
        )
        for i in range(4)
    ]


def start(copies):
    for copy in copies:
        copy.start()


def wait(copies):
    for copy in copies:
        copy.wait()


def drain_out(acc, buffer, out_hbm, sems, first):
    copies = pieces(buffer, out_hbm, sems, first)
    for i in range(4):
        for t in range(3):
            block = acc[t, i * 512 : (i + 1) * 512, :]
            buffer[i * 64 : (i + 1) * 64, :, t * 128 : (t + 1) * 128] = block.reshape(64, 8, 128).astype(BF)
        copies[i].start()
    wait(copies)


def dft_kernel(x_hbm, table_hbm, order_ref, out_hbm, acc, x, table, out, sems):
    x_in = pieces(x_hbm, x, sems, 0)
    table_in = pieces(table_hbm, table, sems, 4)
    start(x_in)
    start(table_in)
    wait(x_in)
    for part in range(4):
        table_in[part].wait()
        res = dot(table[part * DEV : (part + 1) * DEV, :], x[...].reshape(NLON, 2 * C))
        interleave(acc, res, part)
    drain_out(acc, out, out_hbm, sems, 8)


def dft(rows, table, earlier):
    return pl.pallas_call(
        dft_kernel,
        out_shape=jax.ShapeDtypeStruct((DEV, 8, C), BF),
        in_specs=[ANY, ANY, ANY],
        out_specs=ANY,
        scratch_shapes=[
            pltpu.VMEM((3, DEV * 8, 128), F32),
            pltpu.VMEM((32, COLS, 2 * C), BF),
            pltpu.VMEM((2 * MW, NLON), BF),
            pltpu.VMEM((DEV, 8, C), BF),
            pltpu.SemaphoreType.DMA((12,)),
        ],
        compiler_params=PARAMS,
        cost_estimate=pl.CostEstimate(flops=1_700_000_000, bytes_accessed=6_000_000, transcendentals=0),
        name="dft",
    )(rows, table, earlier)


def fill_part(acc, buffer, i):
    for t in range(3):
        block = buffer[i * 64 : (i + 1) * 64, :, t * 128 : (t + 1) * 128]
        acc[t, i * 512 : (i + 1) * 512, :] = block.astype(F32).reshape(512, 128)


def inverse_kernel(w_hbm, table_hbm, order_ref, out_hbm, acc, waves, w, table, out, sems):
    w_in = pieces(w_hbm, w, sems, 0)
    table_in = pieces(table_hbm, table, sems, 4)
    copies = pieces(out, out_hbm, sems, 8)
    start(w_in)
    start(table_in)
    for i in range(4):
        w_in[i].wait()
        fill_part(acc, w, i)
    for part in range(4):
        for a in range(2):
            for t in range(3):
                lane = a * C + t * 128
                waves[part * DEV : (part + 1) * DEV, lane : lane + 128] = picked(acc, a, part, t)
    for i in range(4):
        table_in[i].wait()
        res = dot(table[i * 256 : (i + 1) * 256, :], waves[...])
        out[i * 8 : (i + 1) * 8] = res.astype(BF).reshape(8, COLS, 2 * C)
        copies[i].start()
    wait(copies)


def inverse_dft(waves, table, earlier):
    return pl.pallas_call(
        inverse_kernel,
        out_shape=jax.ShapeDtypeStruct((32, COLS, 2 * C), BF),
        in_specs=[ANY, ANY, ANY],
        out_specs=ANY,
        scratch_shapes=[
            pltpu.VMEM((3, DEV * 8, 128), F32),
            pltpu.VMEM((2 * MW, 2 * C), BF),
            pltpu.VMEM((DEV, 8, C), BF),
            pltpu.VMEM((NLON, 2 * MW), BF),
            pltpu.VMEM((32, COLS, 2 * C), BF),
            pltpu.SemaphoreType.DMA((12,)),
        ],
        compiler_params=PARAMS,
        cost_estimate=pl.CostEstimate(flops=1_700_000_000, bytes_accessed=6_000_000, transcendentals=0),
        name="inverse_dft",
    )(waves, table, earlier)


def spectral_kernel(
    w_hbm, ana_hbm, syn_hbm, sw_hbm, order_ref, out_hbm, acc, waves, mixer, w, ana, syn, sw, sems
):
    w_in = pieces(w_hbm, w, sems, 0)
    ana_in = [pltpu.make_async_copy(ana_hbm.at[m], ana.at[m], sems.at[8 + m]) for m in range(2)]
    syn_in = [pltpu.make_async_copy(syn_hbm.at[m], syn.at[m], sems.at[10 + m]) for m in range(2)]
    sw_in = pltpu.make_async_copy(sw_hbm, sw, sems.at[12])
    start(w_in)
    start(ana_in)
    sw_in.start()
    start(syn_in)
    for i in range(4):
        w_in[i].wait()
        fill_part(acc, w, i)
    for m in range(2):
        for p in range(2):
            for a in range(2):
                for t in range(3):
                    lane = p * C + t * 128
                    waves[m, a * DEV : (a + 1) * DEV, lane : lane + 128] = picked(acc, a, m * 2 + p, t)
    sw_in.wait()
    mixer[:C, :C] = sw[0]
    mixer[:C, C:] = sw[1]
    mixer[C:, :C] = -sw[1]
    mixer[C:, C:] = sw[0]
    for m in range(2):
        ana_in[m].wait()
        coeff = dot(ana[m], waves[m]).astype(BF)
        mixed = dot(coeff, mixer[...]).astype(BF)
        syn_in[m].wait()
        grid = dot(syn[m], mixed, TN)
        for p in range(2):
            for a in range(2):
                for t in range(3):
                    lane = p * C + t * 128
                    acc[t, pl.ds(a * 4 + m * 2 + p, DEV, stride=8), :] = grid[
                        a * DEV : (a + 1) * DEV, lane : lane + 128
                    ]
    drain_out(acc, w, out_hbm, sems, 4)


def spectral_mix(waves, analysis, synthesis, spec_weight, earlier):
    return pl.pallas_call(
        spectral_kernel,
        out_shape=jax.ShapeDtypeStruct((DEV, 8, C), BF),
        in_specs=[ANY] * 5,
        out_specs=ANY,
        scratch_shapes=[
            pltpu.VMEM((3, DEV * 8, 128), F32),
            pltpu.VMEM((2, NLAT, 2 * C), BF),
            pltpu.VMEM((2 * C, 2 * C), BF),
            pltpu.VMEM((DEV, 8, C), BF),
            pltpu.VMEM((2, MW, NLAT), BF),
            pltpu.VMEM((2, MW, NLAT), BF),
            pltpu.VMEM((2, C, C), BF),
            pltpu.SemaphoreType.DMA((13,)),
        ],
        compiler_params=PARAMS,
        cost_estimate=pl.CostEstimate(flops=2_900_000_000, bytes_accessed=6_000_000, transcendentals=0),
        name="spectral_mix",
    )(waves, analysis, synthesis, spec_weight, earlier)


def gelu_parts(x):
    t = jnp.tanh(GELU_K * (x + 0.044715 * (x * x * x)))
    return 0.5 * (1.0 + t), t


def finish_kernel(x_ref, s_ref, own_ref, west_ref, w1_ref, w2_ref, rw_ref, out_ref):
    rows = x_ref.shape[0]
    x = x_ref[...].astype(F32).reshape(rows // 2, 2, COLS, C)
    hidden = jnp.stack(
        [x[:, 0] + s_ref[:, :, :C].astype(F32), x[:, 1] + s_ref[:, :, C:].astype(F32)], axis=1
    )
    hidden = hidden.reshape(rows * COLS, C).astype(BF)
    pre = dot(hidden, w1_ref[...])
    act = (pre * gelu_parts(pre)[0]).astype(BF)
    own = own_ref[...].astype(F32).reshape(rows, 2, 16, FL)
    west = own[:, 0] + west_ref[...].astype(F32).reshape(rows, 16, FL)
    returned = jnp.stack([west, own[:, 1]], axis=1).reshape(rows * COLS, FL).astype(BF)
    out = hidden.astype(F32) + dot(act, w2_ref[...]) + dot(returned, rw_ref[...])
    out_ref[...] = out.astype(BF).reshape(rows, COLS, C)


def finish(atm_state, spectral, own, west, mlp_in, mlp_out, return_weight):
    step = 16
    return pl.pallas_call(
        finish_kernel,
        grid=(ROWS // step,),
        out_shape=jax.ShapeDtypeStruct((ROWS, COLS, C), BF),
        in_specs=[
            pl.BlockSpec((step, COLS, C), lambda i: (i, 0, 0)),
            pl.BlockSpec((step // 2, COLS, 2 * C), lambda i: (i, 0, 0)),
            pl.BlockSpec((step * COLS, FL), lambda i: (i, 0)),
            pl.BlockSpec((step * 16, FL), lambda i: (i, 0)),
            pl.BlockSpec((C, HID), lambda i: (0, 0)),
            pl.BlockSpec((HID, C), lambda i: (0, 0)),
            pl.BlockSpec((FL, C), lambda i: (0, 0)),
        ],
        out_specs=pl.BlockSpec((step, COLS, C), lambda i: (i, 0, 0)),
        compiler_params=PARAMS,
        cost_estimate=pl.CostEstimate(flops=2_700_000_000, bytes_accessed=6_000_000, transcendentals=1_600_000),
        name="finish",
    )(atm_state, spectral, own, west, mlp_in, mlp_out, return_weight)


def scatter_kernel(state_ref, sw_ref, wet_ref, point_ref, weight_ref, order_ref, own_ref, east_ref):
    surface = (dot(state_ref[...].reshape(CELLS, OC), sw_ref[...]) * wet_ref[...]).astype(BF)

    def spread(first, count):
        ids = first + lax.broadcasted_iota(jnp.int32, (count, CELLS), 0)
        total = jnp.zeros((count, CELLS), F32)
        for k in range(KOV):
            total = total + jnp.where(ids == point_ref[k : k + 1, :], weight_ref[k : k + 1, :], 0.0)
        return dot(total.astype(BF), surface).astype(BF)

    for i in range(4):
        own_ref[i * 512 : (i + 1) * 512, :] = spread(i * 512, 512)
    for i in range(2):
        east_ref[i * 512 : (i + 1) * 512, :] = spread(POINTS + i * 512, 512)


def scatter(ocean_state, surface_weight, wet_col, points, weights, earlier):
    return pl.pallas_call(
        scatter_kernel,
        in_specs=[pl.BlockSpec(memory_space=pltpu.VMEM)] * 5 + [ANY],
        out_shape=(
            jax.ShapeDtypeStruct((POINTS, FL), BF),
            jax.ShapeDtypeStruct((EAST, FL), BF),
        ),
        compiler_params=PARAMS,
        cost_estimate=pl.CostEstimate(flops=250_000_000, bytes_accessed=1_500_000, transcendentals=0),
        name="scatter",
    )(ocean_state, surface_weight, wet_col, points, weights, earlier)


def gather_kernel(flux_ref, east_ref, state_ref, wet_ref, oin_ref, point_ref, weight_ref, out_ref):
    def pick(first, count, source):
        ids = first + lax.broadcasted_iota(jnp.int32, (CELLS, count), 1)
        total = jnp.zeros((CELLS, count), F32)
        for k in range(KOV):
            total = total + jnp.where(ids == point_ref[:, k : k + 1], weight_ref[:, k : k + 1], 0.0)
        return dot(total.astype(BF), source)

    forcing = jnp.zeros((CELLS, FL), F32)
    for i in range(4):
        forcing = forcing + pick(i * 512, 512, flux_ref[i * 512 : (i + 1) * 512, :])
    for i in range(2):
        forcing = forcing + pick(POINTS + i * 512, 512, east_ref[i * 512 : (i + 1) * 512, :])
    added = dot(forcing.astype(BF), oin_ref[...])
    state = state_ref[...].reshape(CELLS, OC).astype(F32)
    out_ref[...] = ((state + added) * wet_ref[...]).astype(BF).reshape(16, 16, OC)


def gather(flux, east, ocean_state, wet_col, ocean_in, points, weights):
    return pl.pallas_call(
        gather_kernel,
        out_shape=jax.ShapeDtypeStruct((16, 16, OC), BF),
        compiler_params=PARAMS,
        cost_estimate=pl.CostEstimate(flops=250_000_000, bytes_accessed=1_500_000, transcendentals=0),
        name="gather",
    )(flux, east, ocean_state, wet_col, ocean_in, points, weights)


def ocean_kernel(
    at_ref, mix_ref, west_ref, east_ref, south_ref, north_ref, dk_ref, gain_ref, up_ref, down_ref, wet_ref, cot_ref,
    next_ref, keep_ref, send_ref, pad, grad_ref,
):
    pad[0:3] = south_ref[...].astype(F32)
    pad[3:19, 0:3] = west_ref[...].astype(F32)
    pad[3:19, 3:19] = mix_ref[...].astype(F32)
    pad[3:19, 19:22] = east_ref[...].astype(F32)
    pad[19:22] = north_ref[...].astype(F32)
    depth = jnp.zeros((16, 16, OC), F32)
    for j in range(7):
        shifted = pad[:, j : j + 16, :]
        for i in range(7):
            depth = depth + shifted[i : i + 16] * dk_ref[i * 7 + j : i * 7 + j + 1, :].astype(F32).reshape(1, 1, OC)
    depth = depth.reshape(CELLS, OC)
    centred = depth - jnp.mean(depth, axis=-1, keepdims=True)
    variance = jnp.mean(centred * centred, axis=-1, keepdims=True)
    normal = (centred * lax.rsqrt(variance + 1e-06) * gain_ref[...]).astype(BF)
    wet = wet_ref[...]
    cot = (cot_ref[...].reshape(CELLS, OC).astype(F32) * wet).astype(BF)
    total = jnp.zeros((CELLS, OC), F32)
    for h in range(4):
        cut = slice(h * 256, (h + 1) * 256)
        pre = dot(normal, up_ref[:, cut])
        half, t = gelu_parts(pre)
        lifted = (pre * half).astype(BF)
        total = total + dot(lifted, down_ref[cut, :])
        gdown = dot(lifted, cot, TN).astype(BF)
        grad_ref[h * 8 : (h + 1) * 8, 32:, :] = gdown.reshape(8, 32, OC)
        slope = half + 0.5 * pre * (1.0 - t * t) * (GELU_K * (1.0 + 3.0 * 0.044715 * (pre * pre)))
        pre_grad = (dot(cot, down_ref[cut, :], NT) * slope).astype(BF)
        gup = dot(normal, pre_grad, TN).astype(BF)
        grad_ref[:, h * 8 : (h + 1) * 8, :] = gup.reshape(32, 8, 256)
    mix = mix_ref[...].reshape(CELLS, OC).astype(F32)
    next_ref[...] = ((mix + total) * wet).astype(BF).reshape(16, 16, OC)
    deal(grad_ref, at_ref[0], (keep_ref, send_ref))


def ocean(at, mix, west, east, south, north, depth_kernel, gain, up, down, wet_col, cot):
    vmem = pl.BlockSpec(memory_space=pltpu.VMEM)
    return pl.pallas_call(
        ocean_kernel,
        out_shape=(jax.ShapeDtypeStruct((16, 16, OC), BF),)
        + (jax.ShapeDtypeStruct((16, 64, 256), BF),) * 2,
        in_specs=[pl.BlockSpec(memory_space=pltpu.SMEM)] + [vmem] * 11,
        scratch_shapes=[pltpu.VMEM((22, 22, OC), F32), pltpu.VMEM((32, 64, 256), BF)],
        compiler_params=PARAMS,
        cost_estimate=pl.CostEstimate(flops=700_000_000, bytes_accessed=4_000_000, transcendentals=260_000),
        name="ocean",
    )(at, mix, west, east, south, north, depth_kernel.reshape(49, OC), gain.reshape(1, OC), up, down, wet_col, cot)


def deal(source, at, targets):
    count = len(targets)
    size = source.shape[0] // count
    for shift, target in enumerate(targets):
        target[...] = source[pl.ds(lax.rem(at + shift, count) * size, size)]


def reduce_kernel(count, at_ref, *refs):
    parts, outs, total = refs[:count], refs[count:-1], refs[-1]
    value = parts[0][...].astype(F32)
    for part in parts[1:]:
        value = value + part[...].astype(F32)
    total[...] = value.astype(BF)
    deal(total, at_ref[0], outs)


def reduced(at, parts, count, name):
    shape = parts[0].shape
    out = jax.ShapeDtypeStruct((shape[0] // count, *shape[1:]), BF)
    return pl.pallas_call(
        functools.partial(reduce_kernel, len(parts)),
        out_shape=(out,) * count,
        in_specs=[pl.BlockSpec(memory_space=pltpu.SMEM)]
        + [pl.BlockSpec(memory_space=pltpu.VMEM)] * len(parts),
        scratch_shapes=[pltpu.VMEM(shape, BF)],
        compiler_params=PARAMS,
        cost_estimate=pl.CostEstimate(flops=1_000_000, bytes_accessed=1_000_000, transcendentals=0),
        name=name,
    )(at, *parts)


def column_kernel(parts_ref, out_ref):
    total = parts_ref[0].astype(F32)
    for i in range(1, 8):
        total = total + parts_ref[i].astype(F32)
    out_ref[0] = total.astype(BF)


def column_sum(parts):
    return pl.pallas_call(
        column_kernel,
        out_shape=jax.ShapeDtypeStruct((1, 64, 256), BF),
        compiler_params=PARAMS,
        cost_estimate=pl.CostEstimate(flops=1_000_000, bytes_accessed=500_000, transcendentals=0),
        name="column_sum",
    )(parts)


def collect_kernel(at_ref, *refs):
    blocks, out = refs[:-1], refs[-1]
    count = len(blocks)
    size = blocks[0].shape[0]
    for shift, block in enumerate(blocks):
        out[pl.ds(lax.rem(at_ref[0] - shift + count, count) * size, size)] = block[...]


def collected(at, blocks, name):
    shape = blocks[0].shape
    return pl.pallas_call(
        collect_kernel,
        out_shape=jax.ShapeDtypeStruct((shape[0] * len(blocks), *shape[1:]), BF),
        in_specs=[pl.BlockSpec(memory_space=pltpu.SMEM)]
        + [pl.BlockSpec(memory_space=pltpu.VMEM)] * len(blocks),
        compiler_params=PARAMS,
        cost_estimate=pl.CostEstimate(flops=1_000_000, bytes_accessed=1_000_000, transcendentals=0),
        name=name,
    )(at, *blocks)


def unpack_kernel(at_ref, own_ref, other_ref, up_ref, down_ref):
    for shift, block in enumerate((own_ref, other_ref)):
        at = lax.rem(at_ref[0] + shift, 2)
        rows = pl.ds(pl.multiple_of(at * 128, 128), 128)
        for q in range(4):
            piece = block[:, q * 8 : (q + 1) * 8, :].astype(F32)
            up_ref[rows, q * 256 : (q + 1) * 256] = piece.reshape(128, 256)
        rows = pl.ds(pl.multiple_of(at * 512, 512), 512)
        down_ref[rows, :] = block[:, 32:, :].astype(F32).reshape(512, OC)


def unpack(at, blocks):
    return pl.pallas_call(
        unpack_kernel,
        out_shape=(jax.ShapeDtypeStruct((OC, OH), F32), jax.ShapeDtypeStruct((OH, OC), F32)),
        in_specs=[pl.BlockSpec(memory_space=pltpu.SMEM)] + [pl.BlockSpec(memory_space=pltpu.VMEM)] * 2,
        compiler_params=PARAMS,
        cost_estimate=pl.CostEstimate(flops=1_000_000, bytes_accessed=3_000_000, transcendentals=0),
        name="unpack",
    )(at, *blocks)


def dealt(blocks, axis):
    count = len(blocks)
    return [lax.ppermute(blocks[s], axis, ring(count, s)) for s in range(1, count)]


def exchange(x, axes):
    return lax.all_to_all(x, axes, split_axis=0, concat_axis=0, tiled=True)


def after(x, *others):
    return lax.optimization_barrier((x, *others))[0]


def ring(count, distance):
    return [(i, (i + distance) % count) for i in range(count)]


def local(
    atm_state,
    atm_gain,
    spec_weight,
    mlp_in,
    mlp_out,
    flux_weight,
    return_weight,
    ocean_state,
    wet,
    ocean_in,
    depth_kernel,
    ocean_gain,
    ocean_up,
    ocean_down,
    surface_weight,
    intersection_point,
    intersection_weight,
    return_intersection,
    ocean_cot,
):
    lat = lax.axis_index(LAT)
    lon = lax.axis_index(LON)
    dev = (lat * 32 + lon).astype(jnp.int32).reshape(1)
    forward_np, inverse_np = dft_tables()
    forward_table = jnp.asarray(forward_np)
    inverse_table = jnp.asarray(inverse_np)

    at = {axis: lax.axis_index(axis).astype(jnp.int32).reshape(1) for axis in ("x", "y", "core")}
    flux, flux_west = surface_flux(atm_state, flux_weight)
    flux_east = lax.ppermute(flux_west, LON, ring(32, -1))
    msg = norm(atm_state, atm_gain, flux_west)
    rows = exchange(after(msg, flux_east), LON)
    analysis, synthesis = legendre_tables(dev, msg)

    away = intersection_point - POINTS
    points = jnp.where(
        away < 0, intersection_point, POINTS + (away // COLS) * 16 + away % COLS
    ).reshape(CELLS, KOV)
    wet_col = wet.astype(F32).reshape(CELLS, 1)
    mix = gather(
        flux, flux_east, ocean_state, wet_col, ocean_in, points, intersection_weight.reshape(CELLS, KOV)
    )
    west = lax.ppermute(mix[:, 13:], LON, ring(32, 1))
    east = lax.ppermute(mix[:, :3], LON, ring(32, -1))
    wide = lambda rows_of: jnp.concatenate([west[rows_of], mix[rows_of], east[rows_of]], axis=1)
    top, bottom = wide(slice(13, 16)), wide(slice(0, 3))
    top, bottom, rows = lax.optimization_barrier((top, bottom, rows))
    south = lax.ppermute(top, LAT, [(i, i + 1) for i in range(7)])
    north = lax.ppermute(bottom, LAT, [(i + 1, i) for i in range(7)])
    fold = lax.ppermute(top[::-1, ::-1], LON, [(i, 31 - i) for i in range(32)])
    north = jnp.where(lat == 7, fold, north)

    waves = dft(rows, forward_table, analysis)
    waves, south, north = lax.optimization_barrier((waves, south, north))
    by_order = exchange(waves, ALL)

    ocean_next, *blocks = ocean(
        at["core"], mix, west, east, south, north, depth_kernel, ocean_gain, ocean_up, ocean_down, wet_col, ocean_cot
    )
    blocks = reduced(at["x"], blocks[:1] + dealt(blocks, "core"), 4, "sum_core")
    blocks = reduced(at["y"], list(blocks[:1]) + dealt(blocks, "x"), 4, "sum_x")
    (part,) = reduced(at["y"], list(blocks[:1]) + dealt(blocks, "y"), 1, "sum_y")

    parts = exchange(jnp.broadcast_to(part, (8, 64, 256)), COLUMN)
    mixed = spectral_mix(by_order, analysis, synthesis, spec_weight, part)
    mixed, parts = lax.optimization_barrier((mixed, parts))
    by_row = exchange(mixed, ALL)

    own, to_east = scatter(
        ocean_state, surface_weight, wet_col, points.T, return_intersection.reshape(CELLS, KOV).T, mixed
    )
    from_west = lax.ppermute(to_east, LON, ring(32, 1))
    part = column_sum(parts)
    four = collected(at["y"], [part] + dealt([part] * 4, "y"), "all_y")
    half = collected(at["x"], [four] + dealt([four] * 4, "x"), "all_x")
    grad_up, grad_down = unpack(at["core"], [half] + dealt([half] * 2, "core"))

    grid = inverse_dft(by_row, inverse_table, grad_up)
    spectral = exchange(grid, LON)
    atm_next = finish(atm_state, spectral, own, from_west, mlp_in, mlp_out, return_weight)
    return (atm_next, ocean_next, grad_up, grad_down)


LAT = ("zh", "core")
LON = ("y", "zl", "x")
ALL = LAT + LON
COLUMN = ("zh", "zl")


def solution(mesh):
    fine = Mesh(mesh.devices.reshape(4, 2, 4, 2, 4), ALL)
    block = P(LAT, LON)
    whole = P()
    in_specs = (block,) + (whole,) * 6 + (block,) * 2 + (whole,) * 6 + (block,) * 4
    out_specs = (block, block, whole, whole)
    return jax.shard_map(local, mesh=fine, in_specs=in_specs, out_specs=out_specs, check_vma=False)
```

```python
import functools
import math

import jax
import jax.numpy as jnp
import ml_dtypes
import numpy as np
from jax import lax
from jax.experimental import pallas as pl
from jax.experimental.pallas import tpu as pltpu
from jax.sharding import Mesh
from jax.sharding import PartitionSpec as P

C = 384
HID = 768
NLAT = 512
NLON = 1024
MW = 512
FL = 128
OC = 256
OH = 1024
ROWS = 64
COLS = 32
POINTS = ROWS * COLS
EAST = ROWS * 16
CELLS = 256
KOV = 4
DEV = 256
BF = jnp.bfloat16
F32 = jnp.float32
GELU_K = math.sqrt(2.0 / math.pi)

PARAMS = pltpu.CompilerParams(vmem_limit_bytes=56 << 20)

HBM = pl.BlockSpec(memory_space=pltpu.HBM)
VMEM = pl.BlockSpec(memory_space=pltpu.VMEM)

NN = (((1,), (0,)), ((), ()))
NT = (((1,), (1,)), ((), ()))
TN = (((0,), (0,)), ((), ()))


ANY = pl.BlockSpec(memory_space=pl.ANY)


def dot(a, b, dims=NN):
    return lax.dot_general(a, b, dims, preferred_element_type=F32)


def orders_of_device():
    d = np.arange(DEV)
    return np.stack([d, MW - 1 - d], axis=1)


@functools.cache
def dft_tables():
    orders = orders_of_device().T
    lon = np.arange(NLON)
    phase = 2.0 * np.pi * ((orders[:, :, None] * lon) % NLON) / NLON
    forward = np.stack([np.cos(phase), -np.sin(phase)], axis=1) / NLON
    factor = np.where(orders == 0, 1.0, 2.0)[:, None, :, None]
    inverse = np.stack([np.cos(phase), -np.sin(phase)], axis=1) * factor
    forward = forward.reshape(2 * MW, NLON).astype(np.float32).astype(ml_dtypes.bfloat16)
    inverse = inverse.reshape(2 * MW, NLON).T.astype(np.float32).astype(ml_dtypes.bfloat16)
    return forward, np.ascontiguousarray(inverse)


@functools.cache
def legendre_constants():
    orders = orders_of_device().astype(np.float64)
    lat = np.concatenate([np.arange(0, NLAT, 2), np.arange(1, NLAT, 2)])
    theta = np.pi * (lat + 0.5) / NLAT
    k = np.arange(1, MW, dtype=np.float64)
    partial = np.concatenate([[0.0], np.cumsum(np.log((2 * k - 1) / (2 * k)))])
    partial = partial[orders_of_device()]
    log_s = (0.5 * np.log((2 * orders + 1) / (4 * np.pi)) + 0.5 * partial)[:, :, None]
    log_s = log_s + orders[:, :, None] * np.log(np.sin(theta))
    seed = np.where(log_s > -70.0, np.exp(log_s), 0.0).astype(np.float32)
    seed = seed.reshape(DEV, 8, 128)
    cosine = np.tile(np.cos(theta).astype(np.float32).reshape(4, 128), (2, 1))
    quad = (2.0 * np.pi * (np.pi / NLAT) * np.sin(theta)).astype(np.float32).reshape(4, 128)
    degree = np.arange(MW, dtype=np.float64)
    m = orders[:, :, None]
    live = degree >= m + 1
    a = np.sqrt((4 * degree**2 - 1) / np.where(live, degree**2 - m**2, 1.0), where=live, out=np.zeros(live.shape))
    b2 = np.where(live, (degree - 1) ** 2 - m**2, 0.0) / np.where(live, 4 * (degree - 1) ** 2 - 1, 1.0)
    b = np.sqrt(np.maximum(b2, 0.0))
    coef = np.concatenate([a, a * b], axis=1).astype(np.float32)
    return seed, cosine, quad, coef


def legendre_kernel(dev_ref, coef_ref, seed_ref, cos_ref, quad_ref, order_ref, ana_ref, syn_ref, vals):
    dev = dev_ref[0]
    upper = lax.broadcasted_iota(jnp.int32, (8, 128), 0) < 4
    order = jnp.where(upper, dev, MW - 1 - dev)
    seed = seed_ref[0]
    cosine = cos_ref[...]

    def block(i, carry):
        older, newer = carry
        for step in range(16):
            l = i * 16 + step
            a = jnp.where(upper, coef_ref[0, 0, l], coef_ref[0, 1, l]) * cosine
            ab = jnp.where(upper, coef_ref[0, 2, l], coef_ref[0, 3, l])
            value = a * newer - ab * older
            value = jnp.where(order == l, seed, value)
            vals[pl.ds(pl.multiple_of(l * 8, 8), 8), :] = value
            older, newer = newer, value
        return older, newer

    zero = jnp.zeros((8, 128), F32)
    lax.fori_loop(0, MW // 16, block, (zero, zero))
    for m in range(2):
        for jc in range(4):
            table = vals[pl.ds(m * 4 + jc, MW, stride=8), :]
            ana_ref[m, :, jc * 128 : (jc + 1) * 128] = (table * quad_ref[jc : jc + 1, :]).astype(BF)
            syn_ref[m, :, jc * 128 : (jc + 1) * 128] = table.astype(BF)


def legendre_tables(dev, earlier):
    seed, cosine, quad, coef = legendre_constants()
    table = jax.ShapeDtypeStruct((2, MW, NLAT), BF)
    whole = lambda *shape: pl.BlockSpec(shape, lambda i, d: (0,) * len(shape))
    return pl.pallas_call(
        legendre_kernel,
        out_shape=(table, table),
        grid_spec=pltpu.PrefetchScalarGridSpec(
            num_scalar_prefetch=1,
            grid=(1,),
            in_specs=[
                pl.BlockSpec((1, 4, MW), lambda i, d: (d[0], 0, 0), memory_space=pltpu.SMEM),
                pl.BlockSpec((1, 8, 128), lambda i, d: (d[0], 0, 0)),
                whole(8, 128),
                whole(4, 128),
                ANY,
            ],
            out_specs=[whole(2, MW, NLAT), whole(2, MW, NLAT)],
            scratch_shapes=[pltpu.VMEM((MW * 8, 128), F32)],
        ),
        compiler_params=PARAMS,
        cost_estimate=pl.CostEstimate(flops=10_000_000, bytes_accessed=4_000_000, transcendentals=0),
        name="legendre",
    )(dev, jnp.asarray(coef), jnp.asarray(seed), jnp.asarray(cosine), jnp.asarray(quad), earlier)


def pieces(source, target, sems, first, count=4):
    rows = source.shape[0] // count
    return [
        pltpu.make_async_copy(
            source.at[pl.ds(i * rows, rows)], target.at[pl.ds(i * rows, rows)], sems.at[first + i]
        )
        for i in range(count)
    ]


def start(copies):
    for copy in copies:
        copy.start()


def wait(copies):
    for copy in copies:
        copy.wait()


def flux_kernel(x_ref, fw_ref, flux_ref, west_ref):
    x = x_ref[...]
    flux = dot(x.reshape(-1, C), fw_ref[...]).astype(BF)
    flux_ref[...] = flux
    west_ref[...] = flux.reshape(x.shape[0], 2, 16, FL)[:, 0].reshape(-1, FL)


def surface_flux(atm_state, flux_weight):
    step = 16
    return pl.pallas_call(
        flux_kernel,
        grid=(ROWS // step,),
        out_shape=(
            jax.ShapeDtypeStruct((POINTS, FL), BF),
            jax.ShapeDtypeStruct((EAST, FL), BF),
        ),
        in_specs=[
            pl.BlockSpec((step, COLS, C), lambda i: (i, 0, 0)),
            pl.BlockSpec((C, FL), lambda i: (0, 0)),
        ],
        out_specs=[
            pl.BlockSpec((step * COLS, FL), lambda i: (i, 0)),
            pl.BlockSpec((step * 16, FL), lambda i: (i, 0)),
        ],
        compiler_params=PARAMS,
        cost_estimate=pl.CostEstimate(flops=210_000_000, bytes_accessed=2_500_000, transcendentals=0),
        name="flux",
    )(atm_state, flux_weight)


def norm_kernel(x_hbm, gain_ref, order_ref, msg_hbm, x, msg, sems):
    x_in = pieces(x_hbm, x, sems, 0)
    msg_out = pieces(msg, msg_hbm, sems, 4)
    start(x_in)
    for i in range(4):
        x_in[i].wait()
        xf = x[i * 16 : (i + 1) * 16].astype(F32)
        scale = lax.rsqrt(jnp.mean(xf * xf, axis=-1, keepdims=True) + 1e-06)
        normed = (xf * scale * gain_ref[...].reshape(1, 1, C)).astype(BF)
        pairs = normed.reshape(8, 2, COLS, C)
        msg[i * 8 : (i + 1) * 8, :, :C] = pairs[:, 0]
        msg[i * 8 : (i + 1) * 8, :, C:] = pairs[:, 1]
        msg_out[i].start()
    wait(msg_out)


def norm(atm_state, gain, earlier):
    return pl.pallas_call(
        norm_kernel,
        out_shape=jax.ShapeDtypeStruct((ROWS // 2, COLS, 2 * C), BF),
        in_specs=[HBM, VMEM, ANY],
        out_specs=HBM,
        scratch_shapes=[
            pltpu.VMEM((ROWS, COLS, C), BF),
            pltpu.VMEM((ROWS // 2, COLS, 2 * C), BF),
            pltpu.SemaphoreType.DMA((8,)),
        ],
        compiler_params=PARAMS,
        cost_estimate=pl.CostEstimate(flops=10_000_000, bytes_accessed=3_000_000, transcendentals=0),
        name="norm",
    )(atm_state, gain, earlier)


def interleave(acc, matrix, mp):
    for a in range(2):
        for t in range(3):
            lane = a * C + t * 128
            acc[t, pl.ds(a * 4 + mp, DEV, stride=8), :] = matrix[:, lane : lane + 128]


def picked(acc, a, mp, t):
    return acc[t, pl.ds(a * 4 + mp, DEV, stride=8), :].astype(BF)


def drain_out(acc, buffer, out_hbm, sems, first):
    copies = pieces(buffer, out_hbm, sems, first)
    for i in range(4):
        for t in range(3):
            block = acc[t, i * 512 : (i + 1) * 512, :]
            buffer[i * 64 : (i + 1) * 64, :, t * 128 : (t + 1) * 128] = block.reshape(64, 8, 128).astype(BF)
        copies[i].start()
    wait(copies)


def dft_kernel(x_hbm, table_hbm, order_ref, out_hbm, acc, x, table, out, sems):
    x_in = pieces(x_hbm, x, sems, 0)
    table_in = pieces(table_hbm, table, sems, 4)
    start(x_in)
    start(table_in)
    wait(x_in)
    for part in range(4):
        table_in[part].wait()
        res = dot(table[part * DEV : (part + 1) * DEV, :], x[...].reshape(NLON, 2 * C))
        interleave(acc, res, part)
    drain_out(acc, out, out_hbm, sems, 8)


def dft(rows, table, earlier):
    return pl.pallas_call(
        dft_kernel,
        out_shape=jax.ShapeDtypeStruct((DEV, 8, C), BF),
        in_specs=[ANY, ANY, ANY],
        out_specs=ANY,
        scratch_shapes=[
            pltpu.VMEM((3, DEV * 8, 128), F32),
            pltpu.VMEM((32, COLS, 2 * C), BF),
            pltpu.VMEM((2 * MW, NLON), BF),
            pltpu.VMEM((DEV, 8, C), BF),
            pltpu.SemaphoreType.DMA((12,)),
        ],
        compiler_params=PARAMS,
        cost_estimate=pl.CostEstimate(flops=1_700_000_000, bytes_accessed=6_000_000, transcendentals=0),
        name="dft",
    )(rows, table, earlier)


def fill_part(acc, buffer, i):
    for t in range(3):
        block = buffer[i * 64 : (i + 1) * 64, :, t * 128 : (t + 1) * 128]
        acc[t, i * 512 : (i + 1) * 512, :] = block.astype(F32).reshape(512, 128)


def inverse_kernel(w_hbm, table_hbm, order_ref, out_hbm, acc, waves, w, table, out, sems):
    w_in = pieces(w_hbm, w, sems, 0)
    table_in = pieces(table_hbm, table, sems, 4)
    copies = pieces(out, out_hbm, sems, 8)
    start(w_in)
    start(table_in)
    for i in range(4):
        w_in[i].wait()
        fill_part(acc, w, i)
    for part in range(4):
        for a in range(2):
            for t in range(3):
                lane = a * C + t * 128
                waves[part * DEV : (part + 1) * DEV, lane : lane + 128] = picked(acc, a, part, t)
    for i in range(4):
        table_in[i].wait()
        res = dot(table[i * 256 : (i + 1) * 256, :], waves[...])
        out[i * 8 : (i + 1) * 8] = res.astype(BF).reshape(8, COLS, 2 * C)
        copies[i].start()
    wait(copies)


def inverse_dft(waves, table, earlier):
    return pl.pallas_call(
        inverse_kernel,
        out_shape=jax.ShapeDtypeStruct((32, COLS, 2 * C), BF),
        in_specs=[ANY, ANY, ANY],
        out_specs=ANY,
        scratch_shapes=[
            pltpu.VMEM((3, DEV * 8, 128), F32),
            pltpu.VMEM((2 * MW, 2 * C), BF),
            pltpu.VMEM((DEV, 8, C), BF),
            pltpu.VMEM((NLON, 2 * MW), BF),
            pltpu.VMEM((32, COLS, 2 * C), BF),
            pltpu.SemaphoreType.DMA((12,)),
        ],
        compiler_params=PARAMS,
        cost_estimate=pl.CostEstimate(flops=1_700_000_000, bytes_accessed=6_000_000, transcendentals=0),
        name="inverse_dft",
    )(waves, table, earlier)


def spectral_kernel(
    w_hbm, ana_hbm, syn_hbm, sw_hbm, order_ref, out_hbm, acc, waves, mixer, w, ana, syn, sw, sems
):
    w_in = pieces(w_hbm, w, sems, 0)
    ana_in = [pltpu.make_async_copy(ana_hbm.at[m], ana.at[m], sems.at[8 + m]) for m in range(2)]
    syn_in = [pltpu.make_async_copy(syn_hbm.at[m], syn.at[m], sems.at[10 + m]) for m in range(2)]
    sw_in = pltpu.make_async_copy(sw_hbm, sw, sems.at[12])
    start(w_in)
    start(ana_in)
    sw_in.start()
    start(syn_in)
    for i in range(4):
        w_in[i].wait()
        fill_part(acc, w, i)
    for m in range(2):
        for p in range(2):
            for a in range(2):
                for t in range(3):
                    lane = p * C + t * 128
                    waves[m, a * DEV : (a + 1) * DEV, lane : lane + 128] = picked(acc, a, m * 2 + p, t)
    sw_in.wait()
    mixer[:C, :C] = sw[0]
    mixer[:C, C:] = sw[1]
    mixer[C:, :C] = -sw[1]
    mixer[C:, C:] = sw[0]
    for m in range(2):
        ana_in[m].wait()
        coeff = dot(ana[m], waves[m]).astype(BF)
        mixed = dot(coeff, mixer[...]).astype(BF)
        syn_in[m].wait()
        grid = dot(syn[m], mixed, TN)
        for p in range(2):
            for a in range(2):
                for t in range(3):
                    lane = p * C + t * 128
                    acc[t, pl.ds(a * 4 + m * 2 + p, DEV, stride=8), :] = grid[
                        a * DEV : (a + 1) * DEV, lane : lane + 128
                    ]
    drain_out(acc, w, out_hbm, sems, 4)


def spectral_mix(waves, analysis, synthesis, spec_weight, earlier):
    return pl.pallas_call(
        spectral_kernel,
        out_shape=jax.ShapeDtypeStruct((DEV, 8, C), BF),
        in_specs=[ANY] * 5,
        out_specs=ANY,
        scratch_shapes=[
            pltpu.VMEM((3, DEV * 8, 128), F32),
            pltpu.VMEM((2, NLAT, 2 * C), BF),
            pltpu.VMEM((2 * C, 2 * C), BF),
            pltpu.VMEM((DEV, 8, C), BF),
            pltpu.VMEM((2, MW, NLAT), BF),
            pltpu.VMEM((2, MW, NLAT), BF),
            pltpu.VMEM((2, C, C), BF),
            pltpu.SemaphoreType.DMA((13,)),
        ],
        compiler_params=PARAMS,
        cost_estimate=pl.CostEstimate(flops=2_900_000_000, bytes_accessed=6_000_000, transcendentals=0),
        name="spectral_mix",
    )(waves, analysis, synthesis, spec_weight, earlier)


def gelu_parts(x):
    t = jnp.tanh(GELU_K * (x + 0.044715 * (x * x * x)))
    return 0.5 * (1.0 + t), t


def finish_kernel(x_ref, s_ref, own_ref, west_ref, w1_ref, w2_ref, rw_ref, out_ref):
    rows = x_ref.shape[0]
    x = x_ref[...].astype(F32).reshape(rows // 2, 2, COLS, C)
    hidden = jnp.stack(
        [x[:, 0] + s_ref[:, :, :C].astype(F32), x[:, 1] + s_ref[:, :, C:].astype(F32)], axis=1
    )
    hidden = hidden.reshape(rows * COLS, C).astype(BF)
    pre = dot(hidden, w1_ref[...])
    act = (pre * gelu_parts(pre)[0]).astype(BF)
    own = own_ref[...].astype(F32).reshape(rows, 2, 16, FL)
    west = own[:, 0] + west_ref[...].astype(F32).reshape(rows, 16, FL)
    returned = jnp.stack([west, own[:, 1]], axis=1).reshape(rows * COLS, FL).astype(BF)
    out = hidden.astype(F32) + dot(act, w2_ref[...]) + dot(returned, rw_ref[...])
    out_ref[...] = out.astype(BF).reshape(rows, COLS, C)


def finish(atm_state, spectral, own, west, mlp_in, mlp_out, return_weight):
    step = 16
    return pl.pallas_call(
        finish_kernel,
        grid=(ROWS // step,),
        out_shape=jax.ShapeDtypeStruct((ROWS, COLS, C), BF),
        in_specs=[
            pl.BlockSpec((step, COLS, C), lambda i: (i, 0, 0)),
            pl.BlockSpec((step // 2, COLS, 2 * C), lambda i: (i, 0, 0)),
            pl.BlockSpec((step * COLS, FL), lambda i: (i, 0)),
            pl.BlockSpec((step * 16, FL), lambda i: (i, 0)),
            pl.BlockSpec((C, HID), lambda i: (0, 0)),
            pl.BlockSpec((HID, C), lambda i: (0, 0)),
            pl.BlockSpec((FL, C), lambda i: (0, 0)),
        ],
        out_specs=pl.BlockSpec((step, COLS, C), lambda i: (i, 0, 0)),
        compiler_params=PARAMS,
        cost_estimate=pl.CostEstimate(flops=2_700_000_000, bytes_accessed=6_000_000, transcendentals=1_600_000),
        name="finish",
    )(atm_state, spectral, own, west, mlp_in, mlp_out, return_weight)


def scatter_kernel(state_ref, sw_ref, wet_ref, point_ref, weight_ref, order_ref, own_ref, east_ref):
    surface = (dot(state_ref[...].reshape(CELLS, OC), sw_ref[...]) * wet_ref[...]).astype(BF)

    def spread(first, count):
        ids = first + lax.broadcasted_iota(jnp.int32, (count, CELLS), 0)
        total = jnp.zeros((count, CELLS), F32)
        for k in range(KOV):
            total = total + jnp.where(ids == point_ref[k : k + 1, :], weight_ref[k : k + 1, :], 0.0)
        return dot(total.astype(BF), surface).astype(BF)

    for i in range(4):
        own_ref[i * 512 : (i + 1) * 512, :] = spread(i * 512, 512)
    for i in range(2):
        east_ref[i * 512 : (i + 1) * 512, :] = spread(POINTS + i * 512, 512)


def scatter(ocean_state, surface_weight, wet_col, points, weights, earlier):
    return pl.pallas_call(
        scatter_kernel,
        in_specs=[pl.BlockSpec(memory_space=pltpu.VMEM)] * 5 + [ANY],
        out_shape=(
            jax.ShapeDtypeStruct((POINTS, FL), BF),
            jax.ShapeDtypeStruct((EAST, FL), BF),
        ),
        compiler_params=PARAMS,
        cost_estimate=pl.CostEstimate(flops=250_000_000, bytes_accessed=1_500_000, transcendentals=0),
        name="scatter",
    )(ocean_state, surface_weight, wet_col, points, weights, earlier)


def gather_kernel(flux_ref, east_ref, state_ref, wet_ref, oin_ref, point_ref, weight_ref, out_ref):
    def pick(first, count, source):
        ids = first + lax.broadcasted_iota(jnp.int32, (CELLS, count), 1)
        total = jnp.zeros((CELLS, count), F32)
        for k in range(KOV):
            total = total + jnp.where(ids == point_ref[:, k : k + 1], weight_ref[:, k : k + 1], 0.0)
        return dot(total.astype(BF), source)

    forcing = jnp.zeros((CELLS, FL), F32)
    for i in range(4):
        forcing = forcing + pick(i * 512, 512, flux_ref[i * 512 : (i + 1) * 512, :])
    for i in range(2):
        forcing = forcing + pick(POINTS + i * 512, 512, east_ref[i * 512 : (i + 1) * 512, :])
    added = dot(forcing.astype(BF), oin_ref[...])
    state = state_ref[...].reshape(CELLS, OC).astype(F32)
    out_ref[...] = ((state + added) * wet_ref[...]).astype(BF).reshape(16, 16, OC)


def gather(flux, east, ocean_state, wet_col, ocean_in, points, weights):
    return pl.pallas_call(
        gather_kernel,
        out_shape=jax.ShapeDtypeStruct((16, 16, OC), BF),
        compiler_params=PARAMS,
        cost_estimate=pl.CostEstimate(flops=250_000_000, bytes_accessed=1_500_000, transcendentals=0),
        name="gather",
    )(flux, east, ocean_state, wet_col, ocean_in, points, weights)


def ocean_kernel(
    at_ref, mix_ref, west_ref, east_ref, south_ref, north_ref, dk_ref, gain_ref, up_ref, down_ref, wet_ref, cot_ref,
    next_ref, keep_ref, send_ref, pad, grad_ref,
):
    pad[0:3] = south_ref[...].astype(F32)
    pad[3:19, 0:3] = west_ref[...].astype(F32)
    pad[3:19, 3:19] = mix_ref[...].astype(F32)
    pad[3:19, 19:22] = east_ref[...].astype(F32)
    pad[19:22] = north_ref[...].astype(F32)
    depth = jnp.zeros((16, 16, OC), F32)
    for j in range(7):
        shifted = pad[:, j : j + 16, :]
        for i in range(7):
            depth = depth + shifted[i : i + 16] * dk_ref[i * 7 + j : i * 7 + j + 1, :].astype(F32).reshape(1, 1, OC)
    depth = depth.reshape(CELLS, OC)
    centred = depth - jnp.mean(depth, axis=-1, keepdims=True)
    variance = jnp.mean(centred * centred, axis=-1, keepdims=True)
    normal = (centred * lax.rsqrt(variance + 1e-06) * gain_ref[...]).astype(BF)
    wet = wet_ref[...]
    cot = (cot_ref[...].reshape(CELLS, OC).astype(F32) * wet).astype(BF)
    total = jnp.zeros((CELLS, OC), F32)
    for h in range(4):
        cut = slice(h * 256, (h + 1) * 256)
        pre = dot(normal, up_ref[:, cut])
        half, t = gelu_parts(pre)
        lifted = (pre * half).astype(BF)
        total = total + dot(lifted, down_ref[cut, :])
        gdown = dot(lifted, cot, TN).astype(BF)
        grad_ref[h * 8 : (h + 1) * 8, 32:, :] = gdown.reshape(8, 32, OC)
        slope = half + 0.5 * pre * (1.0 - t * t) * (GELU_K * (1.0 + 3.0 * 0.044715 * (pre * pre)))
        pre_grad = (dot(cot, down_ref[cut, :], NT) * slope).astype(BF)
        gup = dot(normal, pre_grad, TN).astype(BF)
        grad_ref[:, h * 8 : (h + 1) * 8, :] = gup.reshape(32, 8, 256)
    mix = mix_ref[...].reshape(CELLS, OC).astype(F32)
    next_ref[...] = ((mix + total) * wet).astype(BF).reshape(16, 16, OC)
    deal(grad_ref, at_ref[0], (keep_ref, send_ref))


def ocean(at, mix, west, east, south, north, depth_kernel, gain, up, down, wet_col, cot):
    vmem = pl.BlockSpec(memory_space=pltpu.VMEM)
    return pl.pallas_call(
        ocean_kernel,
        out_shape=(jax.ShapeDtypeStruct((16, 16, OC), BF),)
        + (jax.ShapeDtypeStruct((16, 64, 256), BF),) * 2,
        in_specs=[pl.BlockSpec(memory_space=pltpu.SMEM)] + [vmem] * 11,
        scratch_shapes=[pltpu.VMEM((22, 22, OC), F32), pltpu.VMEM((32, 64, 256), BF)],
        compiler_params=PARAMS,
        cost_estimate=pl.CostEstimate(flops=700_000_000, bytes_accessed=4_000_000, transcendentals=260_000),
        name="ocean",
    )(at, mix, west, east, south, north, depth_kernel.reshape(49, OC), gain.reshape(1, OC), up, down, wet_col, cot)


def deal(source, at, targets):
    count = len(targets)
    size = source.shape[0] // count
    for shift, target in enumerate(targets):
        target[...] = source[pl.ds(lax.rem(at + shift, count) * size, size)]


def sum_8_kernel(a_ref, b_ref, c_ref, d_ref, out_ref):
    total = a_ref[0].astype(F32) + b_ref[0].astype(F32) + c_ref[0].astype(F32) + d_ref[0].astype(F32)
    total = total.astype(BF)
    for i in range(8):
        out_ref[i] = total


def sum_8(parts):
    return pl.pallas_call(
        sum_8_kernel,
        out_shape=jax.ShapeDtypeStruct((8, 64, 256), BF),
        compiler_params=PARAMS,
        cost_estimate=pl.CostEstimate(flops=1_000_000, bytes_accessed=1_000_000, transcendentals=0),
        name="sum_y",
    )(*parts)


def reduce_kernel(count, at_ref, *refs):
    parts, outs, total = refs[:count], refs[count:-1], refs[-1]
    value = parts[0][...].astype(F32)
    for part in parts[1:]:
        value = value + part[...].astype(F32)
    total[...] = value.astype(BF)
    deal(total, at_ref[0], outs)


def reduced(at, parts, count, name):
    shape = parts[0].shape
    out = jax.ShapeDtypeStruct((shape[0] // count, *shape[1:]), BF)
    return pl.pallas_call(
        functools.partial(reduce_kernel, len(parts)),
        out_shape=(out,) * count,
        in_specs=[pl.BlockSpec(memory_space=pltpu.SMEM)]
        + [pl.BlockSpec(memory_space=pltpu.VMEM)] * len(parts),
        scratch_shapes=[pltpu.VMEM(shape, BF)],
        compiler_params=PARAMS,
        cost_estimate=pl.CostEstimate(flops=1_000_000, bytes_accessed=1_000_000, transcendentals=0),
        name=name,
    )(at, *parts)


def column_kernel(parts_ref, out_ref):
    total = parts_ref[0].astype(F32)
    for i in range(1, 8):
        total = total + parts_ref[i].astype(F32)
    out_ref[0] = total.astype(BF)


def column_sum(parts):
    return pl.pallas_call(
        column_kernel,
        out_shape=jax.ShapeDtypeStruct((1, 64, 256), BF),
        compiler_params=PARAMS,
        cost_estimate=pl.CostEstimate(flops=1_000_000, bytes_accessed=500_000, transcendentals=0),
        name="column_sum",
    )(parts)


def collect_kernel(at_ref, *refs):
    blocks, out = refs[:-1], refs[-1]
    count = len(blocks)
    size = blocks[0].shape[0]
    for shift, block in enumerate(blocks):
        out[pl.ds(lax.rem(at_ref[0] - shift + count, count) * size, size)] = block[...]


def collected(at, blocks, name):
    shape = blocks[0].shape
    return pl.pallas_call(
        collect_kernel,
        out_shape=jax.ShapeDtypeStruct((shape[0] * len(blocks), *shape[1:]), BF),
        in_specs=[pl.BlockSpec(memory_space=pltpu.SMEM)]
        + [pl.BlockSpec(memory_space=pltpu.VMEM)] * len(blocks),
        compiler_params=PARAMS,
        cost_estimate=pl.CostEstimate(flops=1_000_000, bytes_accessed=1_000_000, transcendentals=0),
        name=name,
    )(at, *blocks)


def unpack_kernel(at_ref, own_ref, other_ref, order_ref, up_ref, down_ref):
    for shift, block in enumerate((own_ref, other_ref)):
        at = lax.rem(at_ref[0] + shift, 2)
        rows = pl.ds(pl.multiple_of(at * 128, 128), 128)
        for q in range(4):
            piece = block[:, q * 8 : (q + 1) * 8, :].astype(F32)
            up_ref[rows, q * 256 : (q + 1) * 256] = piece.reshape(128, 256)
        rows = pl.ds(pl.multiple_of(at * 512, 512), 512)
        down_ref[rows, :] = block[:, 32:, :].astype(F32).reshape(512, OC)


def unpack(at, blocks, earlier):
    return pl.pallas_call(
        unpack_kernel,
        out_shape=(jax.ShapeDtypeStruct((OC, OH), F32), jax.ShapeDtypeStruct((OH, OC), F32)),
        in_specs=[pl.BlockSpec(memory_space=pltpu.SMEM)] + [pl.BlockSpec(memory_space=pltpu.VMEM)] * 2 + [ANY],
        compiler_params=PARAMS,
        cost_estimate=pl.CostEstimate(flops=1_000_000, bytes_accessed=3_000_000, transcendentals=0),
        name="unpack",
    )(at, *blocks, earlier)


def dealt(blocks, axis):
    count = len(blocks)
    return [lax.ppermute(blocks[s], axis, ring(count, s)) for s in range(1, count)]


def exchange(x, axes):
    return lax.all_to_all(x, axes, split_axis=0, concat_axis=0, tiled=True)


def after(x, *others):
    return lax.optimization_barrier((x, *others))[0]


def ring(count, distance):
    return [(i, (i + distance) % count) for i in range(count)]


def local(
    atm_state,
    atm_gain,
    spec_weight,
    mlp_in,
    mlp_out,
    flux_weight,
    return_weight,
    ocean_state,
    wet,
    ocean_in,
    depth_kernel,
    ocean_gain,
    ocean_up,
    ocean_down,
    surface_weight,
    intersection_point,
    intersection_weight,
    return_intersection,
    ocean_cot,
):
    lat = lax.axis_index(LAT)
    lon = lax.axis_index(LON)
    dev = (lat * 32 + lon).astype(jnp.int32).reshape(1)
    forward_np, inverse_np = dft_tables()
    forward_table = jnp.asarray(forward_np)
    inverse_table = jnp.asarray(inverse_np)

    at = {axis: lax.axis_index(axis).astype(jnp.int32).reshape(1) for axis in ("x", "y", "core")}
    flux, flux_west = surface_flux(atm_state, flux_weight)
    flux_east = lax.ppermute(flux_west, LON, ring(32, -1))
    msg = norm(atm_state, atm_gain, flux_west)
    rows = exchange(after(msg, flux_east), LON)

    away = intersection_point - POINTS
    points = jnp.where(
        away < 0, intersection_point, POINTS + (away // COLS) * 16 + away % COLS
    ).reshape(CELLS, KOV)
    wet_col = wet.astype(F32).reshape(CELLS, 1)
    mix = gather(
        flux, flux_east, ocean_state, wet_col, ocean_in, points, intersection_weight.reshape(CELLS, KOV)
    )
    analysis, synthesis = legendre_tables(dev, mix)
    west = lax.ppermute(mix[:, 13:], LON, ring(32, 1))
    east = lax.ppermute(mix[:, :3], LON, ring(32, -1))
    wide = lambda rows_of: jnp.concatenate([west[rows_of], mix[rows_of], east[rows_of]], axis=1)
    top, bottom = wide(slice(13, 16)), wide(slice(0, 3))
    top, bottom, rows = lax.optimization_barrier((top, bottom, rows))
    south = lax.ppermute(top, LAT, [(i, i + 1) for i in range(7)])
    north = lax.ppermute(bottom, LAT, [(i + 1, i) for i in range(7)])
    fold = lax.ppermute(top[::-1, ::-1], LON, [(i, 31 - i) for i in range(32)])
    north = jnp.where(lat == 7, fold, north)

    waves = dft(rows, forward_table, analysis)
    waves, south, north = lax.optimization_barrier((waves, south, north))
    by_order = exchange(waves, ALL)

    ocean_next, *blocks = ocean(
        at["core"], mix, west, east, south, north, depth_kernel, ocean_gain, ocean_up, ocean_down, wet_col, ocean_cot
    )
    blocks = reduced(at["x"], blocks[:1] + dealt(blocks, "core"), 4, "sum_core")
    blocks = reduced(at["y"], list(blocks[:1]) + dealt(blocks, "x"), 4, "sum_x")
    part = sum_8(list(blocks[:1]) + dealt(blocks, "y"))

    parts = exchange(part, COLUMN)
    mixed = spectral_mix(by_order, analysis, synthesis, spec_weight, part)
    mixed, parts = lax.optimization_barrier((mixed, parts))
    by_row = exchange(mixed, ALL)

    own, to_east = scatter(
        ocean_state, surface_weight, wet_col, points.T, return_intersection.reshape(CELLS, KOV).T, mixed
    )
    part = column_sum(parts)
    four = collected(at["y"], [part] + dealt([part] * 4, "y"), "all_y")
    half = collected(at["x"], [four] + dealt([four] * 4, "x"), "all_x")
    grad_up, grad_down = unpack(at["core"], [half] + dealt([half] * 2, "core"), to_east)

    from_west = lax.ppermute(after(to_east, grad_up), LON, ring(32, 1))
    grid = inverse_dft(by_row, inverse_table, grad_up)
    spectral = exchange(after(grid, from_west), LON)
    atm_next = finish(atm_state, spectral, own, from_west, mlp_in, mlp_out, return_weight)
    return (atm_next, ocean_next, grad_up, grad_down)


LAT = ("zh", "core")
LON = ("y", "zl", "x")
ALL = LAT + LON
COLUMN = ("zh", "zl")


def solution(mesh):
    fine = Mesh(mesh.devices.reshape(4, 2, 4, 2, 4), ALL)
    block = P(LAT, LON)
    whole = P()
    in_specs = (block,) + (whole,) * 6 + (block,) * 2 + (whole,) * 6 + (block,) * 4
    out_specs = (block, block, whole, whole)
    return jax.shard_map(local, mesh=fine, in_specs=in_specs, out_specs=out_specs, check_vma=False)
```

```python
import functools
import math

import jax
import jax.numpy as jnp
import ml_dtypes
import numpy as np
from jax import lax
from jax.experimental import pallas as pl
from jax.experimental.pallas import tpu as pltpu
from jax.sharding import Mesh
from jax.sharding import PartitionSpec as P

C = 384
HID = 768
NLAT = 512
NLON = 1024
MW = 512
FL = 128
OC = 256
OH = 1024
ROWS = 64
COLS = 32
POINTS = ROWS * COLS
EAST = ROWS * 16
CELLS = 256
KOV = 4
DEV = 256
BF = jnp.bfloat16
F32 = jnp.float32
GELU_K = math.sqrt(2.0 / math.pi)

PARAMS = pltpu.CompilerParams(vmem_limit_bytes=56 << 20)

HBM = pl.BlockSpec(memory_space=pltpu.HBM)
VMEM = pl.BlockSpec(memory_space=pltpu.VMEM)

NN = (((1,), (0,)), ((), ()))
NT = (((1,), (1,)), ((), ()))
TN = (((0,), (0,)), ((), ()))


ANY = pl.BlockSpec(memory_space=pl.ANY)


def dot(a, b, dims=NN):
    return lax.dot_general(a, b, dims, preferred_element_type=F32)


def orders_of_device():
    d = np.arange(DEV)
    return np.stack([d, MW - 1 - d], axis=1)


@functools.cache
def dft_tables():
    orders = orders_of_device().T
    lon = np.arange(NLON)
    phase = 2.0 * np.pi * ((orders[:, :, None] * lon) % NLON) / NLON
    forward = np.stack([np.cos(phase), -np.sin(phase)], axis=1) / NLON
    factor = np.where(orders == 0, 1.0, 2.0)[:, None, :, None]
    inverse = np.stack([np.cos(phase), -np.sin(phase)], axis=1) * factor
    forward = forward.reshape(2 * MW, NLON).astype(np.float32).astype(ml_dtypes.bfloat16)
    inverse = inverse.reshape(2 * MW, NLON).T.astype(np.float32).astype(ml_dtypes.bfloat16)
    return forward, np.ascontiguousarray(inverse)


@functools.cache
def legendre_constants():
    orders = orders_of_device().astype(np.float64)
    lat = np.concatenate([np.arange(0, NLAT, 2), np.arange(1, NLAT, 2)])
    theta = np.pi * (lat + 0.5) / NLAT
    k = np.arange(1, MW, dtype=np.float64)
    partial = np.concatenate([[0.0], np.cumsum(np.log((2 * k - 1) / (2 * k)))])
    partial = partial[orders_of_device()]
    log_s = (0.5 * np.log((2 * orders + 1) / (4 * np.pi)) + 0.5 * partial)[:, :, None]
    log_s = log_s + orders[:, :, None] * np.log(np.sin(theta))
    seed = np.where(log_s > -70.0, np.exp(log_s), 0.0).astype(np.float32)
    seed = seed.reshape(DEV, 8, 128)
    cosine = np.tile(np.cos(theta).astype(np.float32).reshape(4, 128), (2, 1))
    quad = (2.0 * np.pi * (np.pi / NLAT) * np.sin(theta)).astype(np.float32).reshape(4, 128)
    degree = np.arange(MW, dtype=np.float64)
    m = orders[:, :, None]
    live = degree >= m + 1
    a = np.sqrt((4 * degree**2 - 1) / np.where(live, degree**2 - m**2, 1.0), where=live, out=np.zeros(live.shape))
    b2 = np.where(live, (degree - 1) ** 2 - m**2, 0.0) / np.where(live, 4 * (degree - 1) ** 2 - 1, 1.0)
    b = np.sqrt(np.maximum(b2, 0.0))
    coef = np.concatenate([a, a * b], axis=1).astype(np.float32)
    return seed, cosine, quad, coef


def legendre_kernel(dev_ref, coef_ref, seed_ref, cos_ref, quad_ref, order_ref, ana_ref, syn_ref, vals):
    dev = dev_ref[0]
    upper = lax.broadcasted_iota(jnp.int32, (8, 128), 0) < 4
    order = jnp.where(upper, dev, MW - 1 - dev)
    seed = seed_ref[0]
    cosine = cos_ref[...]

    def block(i, carry):
        older, newer = carry
        for step in range(16):
            l = i * 16 + step
            a = jnp.where(upper, coef_ref[0, 0, l], coef_ref[0, 1, l]) * cosine
            ab = jnp.where(upper, coef_ref[0, 2, l], coef_ref[0, 3, l])
            value = a * newer - ab * older
            value = jnp.where(order == l, seed, value)
            vals[pl.ds(pl.multiple_of(l * 8, 8), 8), :] = value
            older, newer = newer, value
        return older, newer

    zero = jnp.zeros((8, 128), F32)
    lax.fori_loop(0, MW // 16, block, (zero, zero))
    for m in range(2):
        for jc in range(4):
            table = vals[pl.ds(m * 4 + jc, MW, stride=8), :]
            ana_ref[m, :, jc * 128 : (jc + 1) * 128] = (table * quad_ref[jc : jc + 1, :]).astype(BF)
            syn_ref[m, :, jc * 128 : (jc + 1) * 128] = table.astype(BF)


def legendre_tables(dev, earlier):
    seed, cosine, quad, coef = legendre_constants()
    table = jax.ShapeDtypeStruct((2, MW, NLAT), BF)
    whole = lambda *shape: pl.BlockSpec(shape, lambda i, d: (0,) * len(shape))
    return pl.pallas_call(
        legendre_kernel,
        out_shape=(table, table),
        grid_spec=pltpu.PrefetchScalarGridSpec(
            num_scalar_prefetch=1,
            grid=(1,),
            in_specs=[
                pl.BlockSpec((1, 4, MW), lambda i, d: (d[0], 0, 0), memory_space=pltpu.SMEM),
                pl.BlockSpec((1, 8, 128), lambda i, d: (d[0], 0, 0)),
                whole(8, 128),
                whole(4, 128),
                ANY,
            ],
            out_specs=[whole(2, MW, NLAT), whole(2, MW, NLAT)],
            scratch_shapes=[pltpu.VMEM((MW * 8, 128), F32)],
        ),
        compiler_params=PARAMS,
        cost_estimate=pl.CostEstimate(flops=10_000_000, bytes_accessed=4_000_000, transcendentals=0),
        name="legendre",
    )(dev, jnp.asarray(coef), jnp.asarray(seed), jnp.asarray(cosine), jnp.asarray(quad), earlier)


def pieces(source, target, sems, first, count=4):
    rows = source.shape[0] // count
    return [
        pltpu.make_async_copy(
            source.at[pl.ds(i * rows, rows)], target.at[pl.ds(i * rows, rows)], sems.at[first + i]
        )
        for i in range(count)
    ]


def start(copies):
    for copy in copies:
        copy.start()


def wait(copies):
    for copy in copies:
        copy.wait()


def flux_kernel(x_ref, fw_ref, flux_ref, west_ref):
    x = x_ref[...]
    flux = dot(x.reshape(-1, C), fw_ref[...]).astype(BF)
    flux_ref[...] = flux
    west_ref[...] = flux.reshape(x.shape[0], 2, 16, FL)[:, 0].reshape(-1, FL)


def surface_flux(atm_state, flux_weight):
    step = 16
    return pl.pallas_call(
        flux_kernel,
        grid=(ROWS // step,),
        out_shape=(
            jax.ShapeDtypeStruct((POINTS, FL), BF),
            jax.ShapeDtypeStruct((EAST, FL), BF),
        ),
        in_specs=[
            pl.BlockSpec((step, COLS, C), lambda i: (i, 0, 0)),
            pl.BlockSpec((C, FL), lambda i: (0, 0)),
        ],
        out_specs=[
            pl.BlockSpec((step * COLS, FL), lambda i: (i, 0)),
            pl.BlockSpec((step * 16, FL), lambda i: (i, 0)),
        ],
        compiler_params=PARAMS,
        cost_estimate=pl.CostEstimate(flops=210_000_000, bytes_accessed=2_500_000, transcendentals=0),
        name="flux",
    )(atm_state, flux_weight)


def norm_kernel(x_hbm, gain_ref, order_ref, msg_hbm, x, msg, sems):
    x_in = pieces(x_hbm, x, sems, 0)
    msg_out = pieces(msg, msg_hbm, sems, 4)
    start(x_in)
    for i in range(4):
        x_in[i].wait()
        xf = x[i * 16 : (i + 1) * 16].astype(F32)
        scale = lax.rsqrt(jnp.mean(xf * xf, axis=-1, keepdims=True) + 1e-06)
        normed = (xf * scale * gain_ref[...].reshape(1, 1, C)).astype(BF)
        pairs = normed.reshape(8, 2, COLS, C)
        msg[i * 8 : (i + 1) * 8, :, :C] = pairs[:, 0]
        msg[i * 8 : (i + 1) * 8, :, C:] = pairs[:, 1]
        msg_out[i].start()
    wait(msg_out)


def norm(atm_state, gain, earlier):
    return pl.pallas_call(
        norm_kernel,
        out_shape=jax.ShapeDtypeStruct((ROWS // 2, COLS, 2 * C), BF),
        in_specs=[HBM, VMEM, ANY],
        out_specs=HBM,
        scratch_shapes=[
            pltpu.VMEM((ROWS, COLS, C), BF),
            pltpu.VMEM((ROWS // 2, COLS, 2 * C), BF),
            pltpu.SemaphoreType.DMA((8,)),
        ],
        compiler_params=PARAMS,
        cost_estimate=pl.CostEstimate(flops=10_000_000, bytes_accessed=3_000_000, transcendentals=0),
        name="norm",
    )(atm_state, gain, earlier)


def interleave(acc, matrix, mp):
    for a in range(2):
        for t in range(3):
            lane = a * C + t * 128
            acc[t, pl.ds(a * 4 + mp, DEV, stride=8), :] = matrix[:, lane : lane + 128]


def picked(acc, a, mp, t):
    return acc[t, pl.ds(a * 4 + mp, DEV, stride=8), :].astype(BF)


def drain_out(acc, buffer, out_hbm, sems, first):
    copies = pieces(buffer, out_hbm, sems, first)
    for i in range(4):
        for t in range(3):
            block = acc[t, i * 512 : (i + 1) * 512, :]
            buffer[i * 64 : (i + 1) * 64, :, t * 128 : (t + 1) * 128] = block.reshape(64, 8, 128).astype(BF)
        copies[i].start()
    wait(copies)


def dft_kernel(x_hbm, table_hbm, order_ref, out_hbm, acc, x, table, out, sems):
    x_in = pieces(x_hbm, x, sems, 0)
    table_in = pieces(table_hbm, table, sems, 4)
    start(x_in)
    start(table_in)
    wait(x_in)
    for part in range(4):
        table_in[part].wait()
        res = dot(table[part * DEV : (part + 1) * DEV, :], x[...].reshape(NLON, 2 * C))
        interleave(acc, res, part)
    drain_out(acc, out, out_hbm, sems, 8)


def dft(rows, table, earlier):
    return pl.pallas_call(
        dft_kernel,
        out_shape=jax.ShapeDtypeStruct((DEV, 8, C), BF),
        in_specs=[ANY, ANY, ANY],
        out_specs=ANY,
        scratch_shapes=[
            pltpu.VMEM((3, DEV * 8, 128), F32),
            pltpu.VMEM((32, COLS, 2 * C), BF),
            pltpu.VMEM((2 * MW, NLON), BF),
            pltpu.VMEM((DEV, 8, C), BF),
            pltpu.SemaphoreType.DMA((12,)),
        ],
        compiler_params=PARAMS,
        cost_estimate=pl.CostEstimate(flops=1_700_000_000, bytes_accessed=6_000_000, transcendentals=0),
        name="dft",
    )(rows, table, earlier)


def fill_part(acc, buffer, i):
    for t in range(3):
        block = buffer[i * 64 : (i + 1) * 64, :, t * 128 : (t + 1) * 128]
        acc[t, i * 512 : (i + 1) * 512, :] = block.astype(F32).reshape(512, 128)


def inverse_kernel(w_hbm, table_hbm, order_ref, out_hbm, acc, waves, w, table, out, sems):
    w_in = pieces(w_hbm, w, sems, 0)
    table_in = pieces(table_hbm, table, sems, 4)
    copies = pieces(out, out_hbm, sems, 8)
    start(w_in)
    start(table_in)
    for i in range(4):
        w_in[i].wait()
        fill_part(acc, w, i)
    for part in range(4):
        for a in range(2):
            for t in range(3):
                lane = a * C + t * 128
                waves[part * DEV : (part + 1) * DEV, lane : lane + 128] = picked(acc, a, part, t)
    for i in range(4):
        table_in[i].wait()
        res = dot(table[i * 256 : (i + 1) * 256, :], waves[...])
        out[i * 8 : (i + 1) * 8] = res.astype(BF).reshape(8, COLS, 2 * C)
        copies[i].start()
    wait(copies)


def inverse_dft(waves, table, earlier):
    return pl.pallas_call(
        inverse_kernel,
        out_shape=jax.ShapeDtypeStruct((32, COLS, 2 * C), BF),
        in_specs=[ANY, ANY, ANY],
        out_specs=ANY,
        scratch_shapes=[
            pltpu.VMEM((3, DEV * 8, 128), F32),
            pltpu.VMEM((2 * MW, 2 * C), BF),
            pltpu.VMEM((DEV, 8, C), BF),
            pltpu.VMEM((NLON, 2 * MW), BF),
            pltpu.VMEM((32, COLS, 2 * C), BF),
            pltpu.SemaphoreType.DMA((12,)),
        ],
        compiler_params=PARAMS,
        cost_estimate=pl.CostEstimate(flops=1_700_000_000, bytes_accessed=6_000_000, transcendentals=0),
        name="inverse_dft",
    )(waves, table, earlier)


def spectral_kernel(
    w_hbm, ana_hbm, syn_hbm, sw_hbm, order_ref, out_hbm, acc, waves, mixer, w, ana, syn, sw, sems
):
    w_in = pieces(w_hbm, w, sems, 0)
    ana_in = [pltpu.make_async_copy(ana_hbm.at[m], ana.at[m], sems.at[8 + m]) for m in range(2)]
    syn_in = [pltpu.make_async_copy(syn_hbm.at[m], syn.at[m], sems.at[10 + m]) for m in range(2)]
    sw_in = pltpu.make_async_copy(sw_hbm, sw, sems.at[12])
    start(w_in)
    start(ana_in)
    sw_in.start()
    start(syn_in)
    for i in range(4):
        w_in[i].wait()
        fill_part(acc, w, i)
    for m in range(2):
        for p in range(2):
            for a in range(2):
                for t in range(3):
                    lane = p * C + t * 128
                    waves[m, a * DEV : (a + 1) * DEV, lane : lane + 128] = picked(acc, a, m * 2 + p, t)
    sw_in.wait()
    mixer[:C, :C] = sw[0]
    mixer[:C, C:] = sw[1]
    mixer[C:, :C] = -sw[1]
    mixer[C:, C:] = sw[0]
    for m in range(2):
        ana_in[m].wait()
        coeff = dot(ana[m], waves[m]).astype(BF)
        mixed = dot(coeff, mixer[...]).astype(BF)
        syn_in[m].wait()
        grid = dot(syn[m], mixed, TN)
        for p in range(2):
            for a in range(2):
                for t in range(3):
                    lane = p * C + t * 128
                    acc[t, pl.ds(a * 4 + m * 2 + p, DEV, stride=8), :] = grid[
                        a * DEV : (a + 1) * DEV, lane : lane + 128
                    ]
    drain_out(acc, w, out_hbm, sems, 4)


def spectral_mix(waves, analysis, synthesis, spec_weight, earlier):
    return pl.pallas_call(
        spectral_kernel,
        out_shape=jax.ShapeDtypeStruct((DEV, 8, C), BF),
        in_specs=[ANY] * 5,
        out_specs=ANY,
        scratch_shapes=[
            pltpu.VMEM((3, DEV * 8, 128), F32),
            pltpu.VMEM((2, NLAT, 2 * C), BF),
            pltpu.VMEM((2 * C, 2 * C), BF),
            pltpu.VMEM((DEV, 8, C), BF),
            pltpu.VMEM((2, MW, NLAT), BF),
            pltpu.VMEM((2, MW, NLAT), BF),
            pltpu.VMEM((2, C, C), BF),
            pltpu.SemaphoreType.DMA((13,)),
        ],
        compiler_params=PARAMS,
        cost_estimate=pl.CostEstimate(flops=2_900_000_000, bytes_accessed=6_000_000, transcendentals=0),
        name="spectral_mix",
    )(waves, analysis, synthesis, spec_weight, earlier)


def gelu_parts(x):
    t = jnp.tanh(GELU_K * (x + 0.044715 * (x * x * x)))
    return 0.5 * (1.0 + t), t


def finish_kernel(x_ref, s_ref, own_ref, west_ref, w1_ref, w2_ref, rw_ref, out_ref):
    rows = x_ref.shape[0]
    x = x_ref[...].astype(F32).reshape(rows // 2, 2, COLS, C)
    hidden = jnp.stack(
        [x[:, 0] + s_ref[:, :, :C].astype(F32), x[:, 1] + s_ref[:, :, C:].astype(F32)], axis=1
    )
    hidden = hidden.reshape(rows * COLS, C).astype(BF)
    pre = dot(hidden, w1_ref[...])
    act = (pre * gelu_parts(pre)[0]).astype(BF)
    own = own_ref[...].astype(F32).reshape(rows, 2, 16, FL)
    west = own[:, 0] + west_ref[...].astype(F32).reshape(rows, 16, FL)
    returned = jnp.stack([west, own[:, 1]], axis=1).reshape(rows * COLS, FL).astype(BF)
    out = hidden.astype(F32) + dot(act, w2_ref[...]) + dot(returned, rw_ref[...])
    out_ref[...] = out.astype(BF).reshape(rows, COLS, C)


def finish(atm_state, spectral, own, west, mlp_in, mlp_out, return_weight):
    step = 16
    return pl.pallas_call(
        finish_kernel,
        grid=(ROWS // step,),
        out_shape=jax.ShapeDtypeStruct((ROWS, COLS, C), BF),
        in_specs=[
            pl.BlockSpec((step, COLS, C), lambda i: (i, 0, 0)),
            pl.BlockSpec((step // 2, COLS, 2 * C), lambda i: (i, 0, 0)),
            pl.BlockSpec((step * COLS, FL), lambda i: (i, 0)),
            pl.BlockSpec((step * 16, FL), lambda i: (i, 0)),
            pl.BlockSpec((C, HID), lambda i: (0, 0)),
            pl.BlockSpec((HID, C), lambda i: (0, 0)),
            pl.BlockSpec((FL, C), lambda i: (0, 0)),
        ],
        out_specs=pl.BlockSpec((step, COLS, C), lambda i: (i, 0, 0)),
        compiler_params=PARAMS,
        cost_estimate=pl.CostEstimate(flops=2_700_000_000, bytes_accessed=6_000_000, transcendentals=1_600_000),
        name="finish",
    )(atm_state, spectral, own, west, mlp_in, mlp_out, return_weight)


def scatter_kernel(state_ref, sw_ref, wet_ref, point_ref, weight_ref, order_ref, own_ref, east_ref):
    surface = (dot(state_ref[...].reshape(CELLS, OC), sw_ref[...]) * wet_ref[...]).astype(BF)

    def spread(first, count):
        ids = first + lax.broadcasted_iota(jnp.int32, (count, CELLS), 0)
        total = jnp.zeros((count, CELLS), F32)
        for k in range(KOV):
            total = total + jnp.where(ids == point_ref[k : k + 1, :], weight_ref[k : k + 1, :], 0.0)
        return dot(total.astype(BF), surface).astype(BF)

    for i in range(4):
        own_ref[i * 512 : (i + 1) * 512, :] = spread(i * 512, 512)
    for i in range(2):
        east_ref[i * 512 : (i + 1) * 512, :] = spread(POINTS + i * 512, 512)


def scatter(ocean_state, surface_weight, wet_col, points, weights, earlier):
    return pl.pallas_call(
        scatter_kernel,
        in_specs=[pl.BlockSpec(memory_space=pltpu.VMEM)] * 5 + [ANY],
        out_shape=(
            jax.ShapeDtypeStruct((POINTS, FL), BF),
            jax.ShapeDtypeStruct((EAST, FL), BF),
        ),
        compiler_params=PARAMS,
        cost_estimate=pl.CostEstimate(flops=250_000_000, bytes_accessed=1_500_000, transcendentals=0),
        name="scatter",
    )(ocean_state, surface_weight, wet_col, points, weights, earlier)


def gather_kernel(flux_ref, east_ref, state_ref, wet_ref, oin_ref, point_ref, weight_ref, out_ref):
    def pick(first, count, source):
        ids = first + lax.broadcasted_iota(jnp.int32, (CELLS, count), 1)
        total = jnp.zeros((CELLS, count), F32)
        for k in range(KOV):
            total = total + jnp.where(ids == point_ref[:, k : k + 1], weight_ref[:, k : k + 1], 0.0)
        return dot(total.astype(BF), source)

    forcing = jnp.zeros((CELLS, FL), F32)
    for i in range(4):
        forcing = forcing + pick(i * 512, 512, flux_ref[i * 512 : (i + 1) * 512, :])
    for i in range(2):
        forcing = forcing + pick(POINTS + i * 512, 512, east_ref[i * 512 : (i + 1) * 512, :])
    added = dot(forcing.astype(BF), oin_ref[...])
    state = state_ref[...].reshape(CELLS, OC).astype(F32)
    out_ref[...] = ((state + added) * wet_ref[...]).astype(BF).reshape(16, 16, OC)


def gather(flux, east, ocean_state, wet_col, ocean_in, points, weights):
    return pl.pallas_call(
        gather_kernel,
        out_shape=jax.ShapeDtypeStruct((16, 16, OC), BF),
        compiler_params=PARAMS,
        cost_estimate=pl.CostEstimate(flops=250_000_000, bytes_accessed=1_500_000, transcendentals=0),
        name="gather",
    )(flux, east, ocean_state, wet_col, ocean_in, points, weights)


def ocean_kernel(
    at_ref, mix_ref, west_ref, east_ref, south_ref, north_ref, dk_ref, gain_ref, up_ref, down_ref, wet_ref, cot_ref,
    next_ref, keep_ref, send_ref, pad, grad_ref,
):
    pad[:, 0:3] = west_ref[...].astype(F32)
    pad[0:3, 3:19] = south_ref[...].astype(F32)
    pad[3:19, 3:19] = mix_ref[...].astype(F32)
    pad[19:22, 3:19] = north_ref[...].astype(F32)
    pad[:, 19:22] = east_ref[...].astype(F32)
    depth = jnp.zeros((16, 16, OC), F32)
    for j in range(7):
        shifted = pad[:, j : j + 16, :]
        for i in range(7):
            depth = depth + shifted[i : i + 16] * dk_ref[i * 7 + j : i * 7 + j + 1, :].astype(F32).reshape(1, 1, OC)
    depth = depth.reshape(CELLS, OC)
    centred = depth - jnp.mean(depth, axis=-1, keepdims=True)
    variance = jnp.mean(centred * centred, axis=-1, keepdims=True)
    normal = (centred * lax.rsqrt(variance + 1e-06) * gain_ref[...]).astype(BF)
    wet = wet_ref[...]
    cot = (cot_ref[...].reshape(CELLS, OC).astype(F32) * wet).astype(BF)
    total = jnp.zeros((CELLS, OC), F32)
    for h in range(4):
        cut = slice(h * 256, (h + 1) * 256)
        pre = dot(normal, up_ref[:, cut])
        half, t = gelu_parts(pre)
        lifted = (pre * half).astype(BF)
        total = total + dot(lifted, down_ref[cut, :])
        gdown = dot(lifted, cot, TN).astype(BF)
        grad_ref[h * 8 : (h + 1) * 8, 32:, :] = gdown.reshape(8, 32, OC)
        slope = half + 0.5 * pre * (1.0 - t * t) * (GELU_K * (1.0 + 3.0 * 0.044715 * (pre * pre)))
        pre_grad = (dot(cot, down_ref[cut, :], NT) * slope).astype(BF)
        gup = dot(normal, pre_grad, TN).astype(BF)
        grad_ref[:, h * 8 : (h + 1) * 8, :] = gup.reshape(32, 8, 256)
    mix = mix_ref[...].reshape(CELLS, OC).astype(F32)
    next_ref[...] = ((mix + total) * wet).astype(BF).reshape(16, 16, OC)
    deal(grad_ref, at_ref[0], (keep_ref, send_ref))


def ocean(at, mix, west, east, south, north, depth_kernel, gain, up, down, wet_col, cot):
    vmem = pl.BlockSpec(memory_space=pltpu.VMEM)
    return pl.pallas_call(
        ocean_kernel,
        out_shape=(jax.ShapeDtypeStruct((16, 16, OC), BF),)
        + (jax.ShapeDtypeStruct((16, 64, 256), BF),) * 2,
        in_specs=[pl.BlockSpec(memory_space=pltpu.SMEM)] + [vmem] * 11,
        scratch_shapes=[pltpu.VMEM((22, 22, OC), F32), pltpu.VMEM((32, 64, 256), BF)],
        compiler_params=PARAMS,
        cost_estimate=pl.CostEstimate(flops=700_000_000, bytes_accessed=4_000_000, transcendentals=260_000),
        name="ocean",
    )(at, mix, west, east, south, north, depth_kernel.reshape(49, OC), gain.reshape(1, OC), up, down, wet_col, cot)


def deal(source, at, targets):
    count = len(targets)
    size = source.shape[0] // count
    for shift, target in enumerate(targets):
        target[...] = source[pl.ds(lax.rem(at + shift, count) * size, size)]


def sum_8_kernel(a_ref, b_ref, c_ref, d_ref, out_ref):
    total = a_ref[0].astype(F32) + b_ref[0].astype(F32) + c_ref[0].astype(F32) + d_ref[0].astype(F32)
    total = total.astype(BF)
    for i in range(8):
        out_ref[i] = total


def sum_8(parts):
    return pl.pallas_call(
        sum_8_kernel,
        out_shape=jax.ShapeDtypeStruct((8, 64, 256), BF),
        compiler_params=PARAMS,
        cost_estimate=pl.CostEstimate(flops=1_000_000, bytes_accessed=1_000_000, transcendentals=0),
        name="sum_y",
    )(*parts)


def reduce_kernel(count, at_ref, *refs):
    parts, outs, total = refs[:count], refs[count:-1], refs[-1]
    value = parts[0][...].astype(F32)
    for part in parts[1:]:
        value = value + part[...].astype(F32)
    total[...] = value.astype(BF)
    deal(total, at_ref[0], outs)


def reduced(at, parts, count, name):
    shape = parts[0].shape
    out = jax.ShapeDtypeStruct((shape[0] // count, *shape[1:]), BF)
    return pl.pallas_call(
        functools.partial(reduce_kernel, len(parts)),
        out_shape=(out,) * count,
        in_specs=[pl.BlockSpec(memory_space=pltpu.SMEM)]
        + [pl.BlockSpec(memory_space=pltpu.VMEM)] * len(parts),
        scratch_shapes=[pltpu.VMEM(shape, BF)],
        compiler_params=PARAMS,
        cost_estimate=pl.CostEstimate(flops=1_000_000, bytes_accessed=1_000_000, transcendentals=0),
        name=name,
    )(at, *parts)


def column_kernel(parts_ref, out_ref):
    total = parts_ref[0].astype(F32)
    for i in range(1, 8):
        total = total + parts_ref[i].astype(F32)
    out_ref[0] = total.astype(BF)


def column_sum(parts):
    return pl.pallas_call(
        column_kernel,
        out_shape=jax.ShapeDtypeStruct((1, 64, 256), BF),
        compiler_params=PARAMS,
        cost_estimate=pl.CostEstimate(flops=1_000_000, bytes_accessed=500_000, transcendentals=0),
        name="column_sum",
    )(parts)


def collect_kernel(at_ref, *refs):
    blocks, out = refs[:-1], refs[-1]
    count = len(blocks)
    size = blocks[0].shape[0]
    for shift, block in enumerate(blocks):
        out[pl.ds(lax.rem(at_ref[0] - shift + count, count) * size, size)] = block[...]


def collected(at, blocks, name):
    shape = blocks[0].shape
    return pl.pallas_call(
        collect_kernel,
        out_shape=jax.ShapeDtypeStruct((shape[0] * len(blocks), *shape[1:]), BF),
        in_specs=[pl.BlockSpec(memory_space=pltpu.SMEM)]
        + [pl.BlockSpec(memory_space=pltpu.VMEM)] * len(blocks),
        compiler_params=PARAMS,
        cost_estimate=pl.CostEstimate(flops=1_000_000, bytes_accessed=1_000_000, transcendentals=0),
        name=name,
    )(at, *blocks)


def unpack_kernel(at_ref, own_ref, other_ref, order_ref, up_ref, down_ref):
    for shift, block in enumerate((own_ref, other_ref)):
        at = lax.rem(at_ref[0] + shift, 2)
        rows = pl.ds(pl.multiple_of(at * 128, 128), 128)
        for q in range(4):
            piece = block[:, q * 8 : (q + 1) * 8, :].astype(F32)
            up_ref[rows, q * 256 : (q + 1) * 256] = piece.reshape(128, 256)
        rows = pl.ds(pl.multiple_of(at * 512, 512), 512)
        down_ref[rows, :] = block[:, 32:, :].astype(F32).reshape(512, OC)


def unpack(at, blocks, earlier):
    return pl.pallas_call(
        unpack_kernel,
        out_shape=(jax.ShapeDtypeStruct((OC, OH), F32), jax.ShapeDtypeStruct((OH, OC), F32)),
        in_specs=[pl.BlockSpec(memory_space=pltpu.SMEM)] + [pl.BlockSpec(memory_space=pltpu.VMEM)] * 2 + [ANY],
        compiler_params=PARAMS,
        cost_estimate=pl.CostEstimate(flops=1_000_000, bytes_accessed=3_000_000, transcendentals=0),
        name="unpack",
    )(at, *blocks, earlier)


def dealt(blocks, axis):
    count = len(blocks)
    return [lax.ppermute(blocks[s], axis, ring(count, s)) for s in range(1, count)]


def exchange(x, axes):
    return lax.all_to_all(x, axes, split_axis=0, concat_axis=0, tiled=True)


def after(x, *others):
    return lax.optimization_barrier((x, *others))[0]


def ring(count, distance):
    return [(i, (i + distance) % count) for i in range(count)]


def local(
    atm_state,
    atm_gain,
    spec_weight,
    mlp_in,
    mlp_out,
    flux_weight,
    return_weight,
    ocean_state,
    wet,
    ocean_in,
    depth_kernel,
    ocean_gain,
    ocean_up,
    ocean_down,
    surface_weight,
    intersection_point,
    intersection_weight,
    return_intersection,
    ocean_cot,
):
    lat = lax.axis_index(LAT)
    lon = lax.axis_index(LON)
    dev = (lat * 32 + lon).astype(jnp.int32).reshape(1)
    forward_np, inverse_np = dft_tables()
    forward_table = jnp.asarray(forward_np)
    inverse_table = jnp.asarray(inverse_np)

    at = {axis: lax.axis_index(axis).astype(jnp.int32).reshape(1) for axis in ("x", "y", "core")}
    flux, flux_west = surface_flux(atm_state, flux_weight)
    flux_east = lax.ppermute(flux_west, LON, ring(32, -1))
    msg = norm(atm_state, atm_gain, flux_west)
    rows = exchange(after(msg, flux_east), LON)

    away = intersection_point - POINTS
    points = jnp.where(
        away < 0, intersection_point, POINTS + (away // COLS) * 16 + away % COLS
    ).reshape(CELLS, KOV)
    wet_col = wet.astype(F32).reshape(CELLS, 1)
    mix = gather(
        flux, flux_east, ocean_state, wet_col, ocean_in, points, intersection_weight.reshape(CELLS, KOV)
    )
    analysis, synthesis = legendre_tables(dev, mix)
    top, bottom = mix[13:], mix[:3]
    south = lax.ppermute(top, LAT, [(i, i + 1) for i in range(7)])
    north = lax.ppermute(bottom, LAT, [(i + 1, i) for i in range(7)])
    fold = lax.ppermute(top[::-1, ::-1], LON, [(i, 31 - i) for i in range(32)])
    north = jnp.where(lat == 7, fold, north)
    tall = lambda cols: jnp.concatenate([south[:, cols], mix[:, cols], north[:, cols]], axis=0)
    right, left = tall(slice(13, 16)), tall(slice(0, 3))
    west = lax.ppermute(right, LON, ring(32, 1))
    east = lax.ppermute(left, LON, ring(32, -1))

    waves = dft(rows, forward_table, analysis)
    waves, west, east = lax.optimization_barrier((waves, west, east))
    by_order = exchange(waves, ALL)

    ocean_next, *blocks = ocean(
        at["core"], mix, west, east, south, north, depth_kernel, ocean_gain, ocean_up, ocean_down, wet_col, ocean_cot
    )
    blocks = reduced(at["x"], blocks[:1] + dealt(blocks, "core"), 4, "sum_core")
    blocks = reduced(at["y"], list(blocks[:1]) + dealt(blocks, "x"), 4, "sum_x")
    part = sum_8(list(blocks[:1]) + dealt(blocks, "y"))

    parts = exchange(part, COLUMN)
    mixed = spectral_mix(by_order, analysis, synthesis, spec_weight, part)
    mixed, parts = lax.optimization_barrier((mixed, parts))
    by_row = exchange(mixed, ALL)

    own, to_east = scatter(
        ocean_state, surface_weight, wet_col, points.T, return_intersection.reshape(CELLS, KOV).T, mixed
    )
    part = column_sum(parts)
    four = collected(at["y"], [part] + dealt([part] * 4, "y"), "all_y")
    half = collected(at["x"], [four] + dealt([four] * 4, "x"), "all_x")
    grad_up, grad_down = unpack(at["core"], [half] + dealt([half] * 2, "core"), to_east)

    from_west = lax.ppermute(after(to_east, grad_up), LON, ring(32, 1))
    grid = inverse_dft(by_row, inverse_table, grad_up)
    spectral = exchange(after(grid, from_west), LON)
    atm_next = finish(atm_state, spectral, own, from_west, mlp_in, mlp_out, return_weight)
    return (atm_next, ocean_next, grad_up, grad_down)


LAT = ("zh", "core")
LON = ("y", "zl", "x")
ALL = LAT + LON
COLUMN = ("zh", "zl")


def solution(mesh):
    fine = Mesh(mesh.devices.reshape(4, 2, 4, 2, 4), ALL)
    block = P(LAT, LON)
    whole = P()
    in_specs = (block,) + (whole,) * 6 + (block,) * 2 + (whole,) * 6 + (block,) * 4
    out_specs = (block, block, whole, whole)
    return jax.shard_map(local, mesh=fine, in_specs=in_specs, out_specs=out_specs, check_vma=False)
```
